256 devices in a mesh: section: 8 (over x, y_lo), expert: 32 (over z, y_hi, core).
Axes of the slice: x: 4, y: 4 (y_hi: 2, y_lo: 2; y = y_hi * 2 + y_lo), z: 8, core: 2. Of those that a mesh axis runs over, the one named last changes fastest.
Arguments:
- act_up: bfloat16 [8, 4096, 3584], P('section', 'expert'), may hold values from -6 to 6
- routes_up: int32 [8, 4096, 1], P('section', 'expert'), may hold values from 0 to 7; in each aligned block of 128 rows (0 to 127, 128 to 255, ..., all dimensions but the last counted through in order) at most 24 rows name the same one
- gates_up: float32 [8, 4096, 1], P('section', 'expert'), may hold values from 0.3 to 1
- saved_down: bfloat16 [8, 4096, 3584], P('section', 'expert'), may hold values from -6 to 6
- grad_down: bfloat16 [8, 4096, 3584], P('section', 'expert'), may hold values from -4 to 4
- routes_down: int32 [8, 4096, 1], P('section', 'expert'), may hold values from 0 to 7; in each aligned block of 128 rows (0 to 127, 128 to 255, ..., all dimensions but the last counted through in order) at most 24 rows name the same one
- gates_down: float32 [8, 4096, 1], P('section', 'expert'), may hold values from 0.3 to 1
- norm_gain: float32 [8, 3584], P('section'), may hold values from 0.1 to 1.9
- w_gate: bfloat16 [8, 32, 3584, 256], P('section', 'expert'), may hold values from -0.09375 to 0.09375
- w_up: bfloat16 [8, 32, 3584, 256], P('section', 'expert'), may hold values from -0.09375 to 0.09375
- w_down: bfloat16 [8, 32, 256, 3584], P('section', 'expert'), may hold values from -0.1875 to 0.1875
Outputs:
- arriving_up: bfloat16 [8, 4096, 3584], P('section', 'expert')
- arriving_down: bfloat16 [8, 4096, 3584], P('section', 'expert')
The draws below stay inside these ranges and needn't reach their ends.
Inputs may be any that keep to these rules, and one draw needn't show every extreme that they name: `routes_up`: among the 128 tokens of one device at one section, no expert is named more than 24 times, a bound that some block reaches; a token names 1 different experts. `routes_down`: among the 128 tokens of one device at one section, no expert is named more than 24 times, a bound that some block reaches; a token names 1 different experts.
All inputs are finite; a program needn't handle non-finite values.
Results may differ from the reference program's by a relative error of at most 0.0059.
Values may be sent and summed in bfloat16 or wider, within the bound.
A program may use at most 128 MiB of HBM per device.

```python
import math
import jax
import jax.numpy as jnp
import numpy as np
from jax import lax

D = 3584
HID = 1024
SLICES = 4
TOP = 1
TOK_DEV = 128
SECTIONS = 8
EXPERTS = 8
HID_DEV = 256
TOKENS = 4096
CAP = 24
N_EXPERT = 32


def row_scaled(key, spread_low, spread_high, base_field):
    row_scale = jnp.exp(jax.random.uniform(key, (SECTIONS, TOKENS, 1), jnp.float32, jnp.log(spread_low), jnp.log(spread_high)))
    return (base_field * row_scale).astype(jnp.bfloat16)


def draw_act_up(key, part):
    key = jax.random.fold_in(key, 17)
    first_key, second_key = jax.random.split(key)
    base_field = jnp.clip(jax.random.normal(first_key, (SECTIONS, TOKENS, D), jnp.float32), -3.0, 3.0)
    return row_scaled(second_key, 0.2, 2.0, base_field)


def draw_saved_down(key, part):
    key = jax.random.fold_in(key, 23)
    first_key, second_key = jax.random.split(key)
    base_field = jnp.clip(jax.random.normal(first_key, (SECTIONS, TOKENS, D), jnp.float32), -3.0, 3.0)
    return row_scaled(second_key, 0.2, 2.0, base_field)


def steps_of(key, extent, pieces, low, largest):
    level = 1.0
    for dim, shards_of in pieces:
        heights = jax.random.uniform(jax.random.fold_in(jax.random.fold_in(key, 6), dim), (shards_of,), jnp.float32, low / len(pieces), largest / len(pieces))
        level = level * jnp.repeat(jnp.exp(heights), extent[dim] // shards_of).reshape((-1,) + (1,) * (len(extent) - 1 - dim))
    return level


def shared_out(own_key, own, number, rows, amount, top, limit, skew):
    sequence = jax.random.permutation(own_key, amount)
    heavy_load, usual = load_shares(amount, rows * top, limit, skew, True), load_shares(amount, rows * top, limit, skew, False)
    places = jnp.arange(amount)

    def named(lengths, turn):
        used = int((lengths > 0).sum())
        fixed = max(1, used // 4)
        moved = fixed + (places - fixed + turn * (used - fixed)) % max(1, amount - fixed)
        return jnp.zeros((amount,), jnp.int32).at[sequence[jnp.where(places < fixed, places, moved)]].set(jnp.asarray(lengths, jnp.int32))

    lengths = jnp.where(number % 4 == 0, named(heavy_load, number // 4), named(usual, number - number // 4 - 1))
    mixed = jax.random.permutation(jax.random.fold_in(own, 3), amount)
    donor, receiver = mixed[0:amount // 2 * 2:2], mixed[1:amount // 2 * 2:2]
    margin = jnp.minimum(lengths[donor] - 1, limit - lengths[receiver]) // 2
    margin = jnp.where((donor == sequence[0]) | (receiver == sequence[0]) | (lengths[receiver] == 0), 0, jnp.maximum(margin, 0))
    moved = jax.random.randint(jax.random.fold_in(own, 4), (amount // 2,), 0, 1 << 20) % (margin + 1)
    lengths = lengths.at[donor].add(-moved).at[receiver].add(moved)
    items = jnp.searchsorted(jnp.cumsum(lengths), jnp.arange(rows * top), side="right").astype(jnp.int32)
    table = items.reshape(top, rows).T
    table = table[jax.random.permutation(jax.random.fold_in(own, 1), rows)]
    turn = jax.random.randint(jax.random.fold_in(own, 2), (rows, 1), 0, top)
    return jnp.take_along_axis(table, (jnp.arange(top)[None, :] + turn) % top, axis=1)


def load_shares(number_of, total, bound, lean, full):
    weights = [(1 << 20) // math.isqrt(rank ** lean) + 1 for rank in range(1, number_of + 1)]
    largest = bound if full else min(bound, max(-(-total // number_of), total * weights[0] // sum(weights)))
    least = 1 if total - largest >= number_of - 1 else 0
    given, spare = [largest] + [least] * (number_of - 1), total - largest - least * (number_of - 1)
    while spare > 0:
        free = [i for i in range(1, number_of) if given[i] < largest] or [i for i in range(1, number_of) if given[i] < bound]
        pool, remaining = sum([weights[i] for i in free]), spare
        for i in free:
            more = min(bound - given[i], max(1, remaining * weights[i] // pool), spare)
            given[i] = given[i] + more
            spare = spare - more
    return np.array(given)


def normal_values(stream_key, extent, spread, bound, pieces=(), held_as=jnp.bfloat16):
    factor_of = steps_of(stream_key, extent, pieces, -0.22, 0.18) if pieces else 1.0
    drawn = jax.random.normal(stream_key, extent, jnp.float32) * spread * factor_of
    return jnp.minimum(jnp.maximum(drawn, -bound), bound).astype(held_as)


def setup_inputs(seed: int = 0) -> dict:
    key_list = jax.random.split(jax.random.key(seed), 12)
    act_up = draw_act_up(jax.random.fold_in(key_list[11], 71), 0)
    routes_up_keys = jax.random.split(jax.random.fold_in(key_list[1], 1), SECTIONS * TOKENS // TOK_DEV)
    routes_up_turns = jax.random.permutation(jax.random.fold_in(key_list[1], 3), SECTIONS * TOKENS // TOK_DEV)
    routes_up = jax.vmap(lambda own, number: shared_out(jax.random.fold_in(key_list[1], 2), own, number, TOK_DEV, EXPERTS, TOP, CAP, 2))(routes_up_keys, routes_up_turns).reshape((SECTIONS, TOKENS, TOP))
    gates_up = jnp.clip(jnp.exp(math.log(1.0) - 1.2039728 * jax.random.uniform(key_list[2], (SECTIONS, TOKENS, TOP), jnp.float32) ** steps_of(key_list[2], (SECTIONS, TOKENS, TOP), ((0, 8), (1, 32)), -0.2, 0.2)), 0.3, 1.0)
    saved_down = draw_saved_down(jax.random.fold_in(key_list[11], 71), 0)
    grad_down = normal_values(key_list[4], (SECTIONS, TOKENS, D), 1.0, 4.0, ((0, 8), (1, 32)))
    routes_down_keys = jax.random.split(jax.random.fold_in(key_list[5], 1), SECTIONS * TOKENS // TOK_DEV)
    routes_down_turns = jax.random.permutation(jax.random.fold_in(key_list[5], 3), SECTIONS * TOKENS // TOK_DEV)
    routes_down = jax.vmap(lambda own, number: shared_out(jax.random.fold_in(key_list[5], 2), own, number, TOK_DEV, EXPERTS, TOP, CAP, 2))(routes_down_keys, routes_down_turns).reshape((SECTIONS, TOKENS, TOP))
    gates_down = jnp.clip(jnp.exp(math.log(1.0) - 1.2039728 * jax.random.uniform(key_list[6], (SECTIONS, TOKENS, TOP), jnp.float32) ** steps_of(key_list[6], (SECTIONS, TOKENS, TOP), ((0, 8), (1, 32)), -0.2, 0.2)), 0.3, 1.0)
    norm_gain = jnp.clip(1.0 + 0.18 * jax.random.normal(key_list[7], (SECTIONS, D), jnp.float32), 0.1, 1.9)
    w_gate = normal_values(key_list[8], (SECTIONS, EXPERTS * SLICES, D, HID_DEV), D ** -0.5, 0.09375, ((0, 8), (1, 32)))
    w_up = normal_values(key_list[9], (SECTIONS, EXPERTS * SLICES, D, HID_DEV), D ** -0.5, 0.09375, ((0, 8), (1, 32)))
    w_down = normal_values(key_list[10], (SECTIONS, EXPERTS * SLICES, HID_DEV, D), HID ** -0.5, 0.1875, ((0, 8), (1, 32)))
    return dict(act_up=act_up, routes_up=routes_up, gates_up=gates_up, saved_down=saved_down, grad_down=grad_down, routes_down=routes_down, gates_down=gates_down, norm_gain=norm_gain, w_gate=w_gate, w_up=w_up, w_down=w_down)


EPS = 1e-06

def normalize(inputs, gain_row):
    values = inputs.astype(jnp.float32)
    scaling = lax.rsqrt(lax.optimization_barrier(jnp.mean(values * values, axis=-1, keepdims=True)) + EPS)
    return (values, scaling, (values * scaling * gain_row).astype(jnp.bfloat16))

def layout(routes):
    entries = routes.reshape(N_EXPERT, TOK_DEV * TOP)
    onehot = (entries[:, :, None] == jnp.arange(EXPERTS, dtype=jnp.int32)[None, None, :]).astype(jnp.int32)
    before = jnp.cumsum(onehot, axis=1) - onehot
    slots = lax.optimization_barrier(jnp.sum(before * onehot, axis=2)).astype(jnp.int32)
    sources = jnp.broadcast_to(jnp.arange(N_EXPERT, dtype=jnp.int32)[:, None], entries.shape)
    return (entries.reshape(-1), sources.reshape(-1), slots.reshape(-1))

def scatter_rows(table, expert_ids, sources, slots):
    buffer = jnp.zeros((EXPERTS, N_EXPERT, CAP, table.shape[-1]), table.dtype)
    buffer = buffer.at[expert_ids, sources, slots].set(table)
    return buffer.reshape(EXPERTS, N_EXPERT * CAP, table.shape[-1])

def expert_forward(buffer, gate_mat, up_mat, down_mat):
    inputs = buffer.astype(jnp.float32)
    gate_act = jnp.einsum('erd,edh->erh', inputs, gate_mat.astype(jnp.float32))
    up_act = jnp.einsum('erd,edh->erh', inputs, up_mat.astype(jnp.float32))
    middle = (jax.nn.silu(gate_act) * up_act).astype(jnp.bfloat16)
    result = jnp.einsum('erh,ehd->erd', middle.astype(jnp.float32), down_mat.astype(jnp.float32))
    return result.astype(jnp.bfloat16)

def expert_backward(buffer, grad_buffer, gate_mat, up_mat, down_mat):
    inputs = buffer.astype(jnp.float32)
    gate_f = gate_mat.astype(jnp.float32)
    up_f = up_mat.astype(jnp.float32)
    gate_act = jnp.einsum('erd,edh->erh', inputs, gate_f)
    up_act = jnp.einsum('erd,edh->erh', inputs, up_f)
    pulled = jnp.einsum('erd,ehd->erh', grad_buffer.astype(jnp.float32), down_mat.astype(jnp.float32))
    sigma_gate = jax.nn.sigmoid(gate_act)
    silu_gate = gate_act * sigma_gate
    d_gate = (pulled * up_act * sigma_gate * (1.0 + gate_act * (1.0 - sigma_gate))).astype(jnp.bfloat16)
    d_upper = (pulled * silu_gate).astype(jnp.bfloat16)
    result = jnp.einsum('erh,edh->erd', d_gate.astype(jnp.float32), gate_f)
    result = result + jnp.einsum('erh,edh->erd', d_upper.astype(jnp.float32), up_f)
    return result.astype(jnp.bfloat16)

def reference(act_up, routes_up, gates_up, saved_down, grad_down, routes_down, gates_down, norm_gain, w_gate, w_up, w_down):
    forward_list = []
    backward_list = []
    for section_index in range(SECTIONS):
        gain_row = norm_gain[section_index]
        gate_all = w_gate[section_index].reshape(SLICES, EXPERTS, D, HID_DEV)
        up_all = w_up[section_index].reshape(SLICES, EXPERTS, D, HID_DEV)
        down_all = w_down[section_index].reshape(SLICES, EXPERTS, HID_DEV, D)
        values_up, scaling_up, normed_up = normalize(act_up[section_index], gain_row)
        values_down, scaling_down, normed_down = normalize(saved_down[section_index], gain_row)
        ids_up, sources_up, slots_up = layout(routes_up[section_index])
        ids_down, sources_down, slots_down = layout(routes_down[section_index])
        buffer_up = scatter_rows(jnp.repeat(normed_up, TOP, axis=0), ids_up, sources_up, slots_up)
        buffer_down = scatter_rows(jnp.repeat(normed_down, TOP, axis=0), ids_down, sources_down, slots_down)
        buffer_grad = scatter_rows(jnp.repeat(grad_down[section_index], TOP, axis=0), ids_down, sources_down, slots_down)
        total_up = jnp.zeros((EXPERTS, N_EXPERT * CAP, D), jnp.float32)
        total_down = jnp.zeros((EXPERTS, N_EXPERT * CAP, D), jnp.float32)
        for slice_index in range(SLICES):
            total_up = total_up + expert_forward(buffer_up, gate_all[slice_index], up_all[slice_index], down_all[slice_index]).astype(jnp.float32)
            total_down = total_down + expert_backward(buffer_down, buffer_grad, gate_all[slice_index], up_all[slice_index], down_all[slice_index]).astype(jnp.float32)
        back_up = total_up.reshape(EXPERTS, N_EXPERT, CAP, D)[ids_up, sources_up, slots_up].reshape(TOKENS, TOP, D)
        back_down = total_down.reshape(EXPERTS, N_EXPERT, CAP, D)[ids_down, sources_down, slots_down].reshape(TOKENS, TOP, D)
        mixed_up = lax.optimization_barrier(jnp.sum(back_up * gates_up[section_index][:, :, None], axis=1))
        forward_list.append((values_up + mixed_up).astype(jnp.bfloat16))
        pulled_in = lax.optimization_barrier(jnp.sum(back_down * gates_down[section_index][:, :, None], axis=1)) * gain_row
        cubed = scaling_down * scaling_down * scaling_down
        result = grad_down[section_index].astype(jnp.float32) + scaling_down * pulled_in
        result = result - values_down * cubed * lax.optimization_barrier(jnp.mean(values_down * pulled_in, axis=-1, keepdims=True))
        backward_list.append(result.astype(jnp.bfloat16))
    arriving_up = jnp.roll(jnp.stack(forward_list), 1, axis=0)
    arriving_down = jnp.roll(jnp.stack(backward_list), -1, axis=0)
    return (arriving_up, arriving_down)
```

```python
import functools

import jax
import jax.numpy as jnp
from jax import lax
from jax.experimental import pallas as pl
from jax.experimental.pallas import tpu as pltpu
from jax.sharding import PartitionSpec as P

EPS = 1e-06
CAP = 24
BLOCK = 2 * CAP
EXPERTS = 8
SLICES = 4
MIB = 1024 * 1024
MESH = pl.DeviceIdType.MESH
F32 = jnp.float32
BF16 = jnp.bfloat16


def nearest(rel):
    inside = lax.rem(rel + 7, 8) // 4
    second = 1 - inside
    dist = second * (rel - 1) + inside * lax.rem(8 - rel, 8)
    return second, dist


def expert_home(zl, yh, c):
    return zl * 4 + yh * 2 + c


def column(row):
    n = row.shape[1]
    eye = lax.broadcasted_iota(jnp.int32, (n, n), 0) == lax.broadcasted_iota(jnp.int32, (n, n), 1)
    return jnp.sum(jnp.where(eye, row, 0.0), axis=1, keepdims=True)


def block_rows(route_row):
    n = route_row.shape[1]
    earlier = lax.broadcasted_iota(jnp.int32, (n, n), 0) < lax.broadcasted_iota(jnp.int32, (n, n), 1)
    same = jnp.logical_and(column(route_row) == route_row, earlier)
    slot = jnp.sum(jnp.where(same, 1.0, 0.0), axis=0, keepdims=True)
    return route_row * float(BLOCK) + slot


def contract_last(a, b):
    return lax.dot_general(a, b, (((1,), (1,)), ((), ())), preferred_element_type=F32)


def kernel(
    act, saved, grad, gain, meta, wg_in, wu_in, wd_in,
    out_up, out_dn,
    wg, wu, wd, table, packed, rows_in, acc_up, acc_dn,
    back_up_out, back_dn_out, back_up_in, back_dn_in,
    act_in, saved_in, grad_in, gain_in, meta_up_in, meta_dn_in,
    row_send, row_recv, src_send, w_recv, sib_send, fwd_send,
    up_send, up_recv, dn_send, dn_recv, res_send, res_recv,
):
    tokens, features = act.shape
    half = features // 2
    hidden = wg_in.shape[1]
    n_sec = lax.axis_size("section")
    sec = lax.axis_index("section")
    me = lax.axis_index("expert")
    z, yh, c = me // 4, lax.rem(me // 2, 2), lax.rem(me, 2)
    after = lax.rem(sec + 1, n_sec)
    before = lax.rem(sec + n_sec - 1, n_sec)

    own_zl = lax.rem(z, 2)
    own_first = 2 * (2 * c + own_zl)
    own_rel = lax.rem(z - own_first + 8, 8)
    own_second, _ = nearest(own_rel)
    own_host = own_first + own_second
    m = own_rel // 2
    own_place = (1 - own_zl) * (m + m // 2 - 2 * (m // 3)) + own_zl * (2 * m - m // 2 - 4 * (m // 3))

    pair = z // 2
    side = lax.rem(z, 2)
    host_zl, host_c = lax.rem(pair, 2), pair // 2
    host_expert = expert_home(host_zl, yh, host_c)
    other_host = (2 * pair + 1 - side) * 4 + yh * 2 + c
    sibling = z * 4 + yh * 2 + 1 - c
    leads_even = 1 - lax.rem(host_zl + side, 2)

    def source(dist, src_yh):
        src_z = lax.rem(2 * pair + side + (2 * side - 1) * dist + 8, 8)
        return src_z * 4 + src_yh * 2 + c

    def host_of(g):
        zl, g_yh, g_c = g // 4, (g // 2) % 2, g % 2
        first = 2 * (2 * g_c + zl)
        second, dist = nearest(lax.rem(z - first + 8, 8))
        return (first + second) * 4 + g_yh * 2 + c, dist * 2 + yh

    def slice_source(place):
        rel = (1 - host_zl) * (0, 2, 6, 4)[place] + host_zl * (1, 7, 3, 5)[place]
        return lax.rem(2 * pair + rel, 8) * 4 + yh * 2 + host_c

    barrier = pltpu.get_barrier_semaphore()

    def greet(section, peer):
        pl.semaphore_signal(barrier, inc=1, device_id=(section, peer), device_id_type=MESH)

    for dist in range(4):
        for src_yh in range(2):
            peer = source(dist, src_yh)

            @pl.when(peer != me)
            def _():
                greet(sec, peer)

    for place in range(4):
        peer = slice_source(place)
        leads = leads_even if place % 2 == 0 else 1 - leads_even

        @pl.when(jnp.logical_and(leads == 1, peer != me))
        def _():
            greet(sec, peer)

    greet(sec, other_host)
    greet(sec, sibling)
    for g in range(EXPERTS):
        peer, _ = host_of(g)
        greet(before, peer)
        greet(after, peer)
    greet(before, me)
    greet(after, me)
    here = jnp.where(own_host == z, 1, 0)
    pl.semaphore_wait(barrier, 29 - here)

    mats = ((wg_in, wg), (wu_in, wu), (wd_in, wd))

    def w_half(ref, index, h):
        size = mats[index][0].shape[0] // 2
        return ref.at[pl.ds(pl.multiple_of(h * size, 128), size)]

    def remote(src, dst, send, recv, section, peer):
        return pltpu.make_async_remote_copy(
            src_ref=src, dst_ref=dst, send_sem=send, recv_sem=recv,
            device_id=(section, peer), device_id_type=MESH,
        )

    def slice_copy(index, h):
        src, dst = mats[index]
        return remote(
            w_half(src, index, h), w_half(dst.at[own_place], index, h),
            src_send.at[index, h], w_recv.at[own_place, index, h], sec, own_host * 4 + yh * 2 + h,
        )

    for index in range(3):
        for h in range(2):
            mine = jnp.logical_and(own_host == z, c == h)

            @pl.when(mine)
            def _():
                src, dst = mats[index]
                pltpu.make_async_copy(
                    w_half(src, index, h), w_half(dst.at[own_place], index, h), w_recv.at[own_place, index, h]
                ).start()

            @pl.when(jnp.logical_not(mine))
            def _():
                slice_copy(index, h).start()

    gain_row = gain[...]
    rows_step = 16

    def norm_rows(step, _):
        at = pl.ds(pl.multiple_of(step * rows_step, rows_step), rows_step)
        for source_ref, base in ((act, 0), (saved, tokens)):
            values = source_ref[at, :].astype(F32)
            scaling = lax.rsqrt(jnp.mean(values * values, axis=-1, keepdims=True) + EPS)
            to = pl.ds(pl.multiple_of(base + step * rows_step, rows_step), rows_step)
            table[to, :features] = (values * scaling * gain_row).astype(BF16)
        return 0

    lax.fori_loop(0, tokens // rows_step, norm_rows, 0)
    table[:tokens, features:] = grad[:, :half]
    table[tokens:, features:] = grad[:, half:]

    at_up = block_rows(meta[0:1, :])
    at_dn = block_rows(meta[2:3, :])
    n_rows = EXPERTS * BLOCK
    row_index = lax.broadcasted_iota(jnp.int32, (n_rows, 2 * tokens), 0).astype(F32)
    pick_h = (row_index == jnp.concatenate([at_up, at_dn + float(CAP)], axis=1)).astype(BF16)
    pick_g = (row_index == jnp.concatenate([at_dn, at_dn + float(CAP)], axis=1)).astype(BF16)
    width = 256

    def pack(first, pick):
        def body(step, _):
            at = pl.ds(pl.multiple_of(first + step * width, width), width)
            packed[:, at] = jnp.dot(pick, table[:, at], preferred_element_type=F32).astype(BF16)
            return 0

        return body

    lax.fori_loop(0, features // width, pack(0, pick_h), 0)
    lax.fori_loop(0, half // width, pack(features, pick_g), 0)

    def row_block(ref, index):
        return ref.at[pl.ds(pl.multiple_of(index * BLOCK, BLOCK), BLOCK)]

    def row_copy(g):
        peer, slot = host_of(g)
        return peer, remote(
            row_block(packed, g), row_block(rows_in, slot), row_send.at[g], row_recv.at[slot], sec, peer
        )

    for g in range(EXPERTS):
        peer, slot = host_of(g)

        @pl.when(peer == me)
        def _():
            pltpu.make_async_copy(row_block(packed, g), row_block(rows_in, slot), row_recv.at[slot]).start()

        @pl.when(peer != me)
        def _():
            row_copy(g)[1].start()

    residuals = [
        remote(act, act_in, res_send.at[0], res_recv.at[0], after, me),
        remote(meta, meta_up_in, res_send.at[1], res_recv.at[1], after, me),
        remote(saved, saved_in, res_send.at[2], res_recv.at[2], before, me),
        remote(grad, grad_in, res_send.at[3], res_recv.at[3], before, me),
        remote(gain, gain_in, res_send.at[4], res_recv.at[4], before, me),
        remote(meta, meta_dn_in, res_send.at[5], res_recv.at[5], before, me),
    ]
    for copy in residuals:
        copy.start()

    acc_up[...] = jnp.zeros_like(acc_up)
    acc_dn[...] = jnp.zeros_like(acc_dn)

    def half_copy(place, index, h, send, peer):
        view = w_half(mats[index][1].at[place], index, h)
        return remote(view, view, send, w_recv.at[place, index, h], sec, peer)

    def sibling_copy(place, index):
        return half_copy(place, index, c, sib_send.at[place, index], sibling)

    def host_copy(place, index):
        return half_copy(place, index, c, fwd_send.at[place, index], other_host)

    def leads_at(place):
        return (leads_even if place % 2 == 0 else 1 - leads_even) == 1

    def forward(place):
        for index in range(3):
            sibling_copy(place, index).wait_recv()

            @pl.when(leads_at(place))
            def _():
                host_copy(place, index).start()

            sibling_copy(place, index).start()

    def wait_sibling(place):
        for index in range(3):
            half_copy(place, index, 1 - c, sib_send.at[place, index], sibling).wait_recv()

    n_src = EXPERTS

    def split(stacked):
        blocks = stacked.reshape(n_src, BLOCK, hidden)
        return (
            blocks[:, :CAP].reshape(n_src * CAP, hidden),
            blocks[:, CAP:].reshape(n_src * CAP, hidden),
        )

    def send_back(acc, out, send, recv, section, into):
        for dist in (3, 2, 1, 0):
            for src_yh in range(2):
                q = dist * 2 + src_yh
                both = jnp.concatenate(
                    [acc[q * CAP:(q + 1) * CAP, :half], acc[q * CAP:(q + 1) * CAP, half:]], axis=0
                )
                out[q * BLOCK:(q + 1) * BLOCK, :] = both.astype(BF16)
                back_copy(q, out, send, recv, section, into).start()

    def back_copy(q, out, send, recv, section, into):
        return remote(
            row_block(out, q), row_block(into, host_expert), send.at[q], recv.at[host_expert],
            section, source(q // 2, q % 2),
        )

    up_args = (back_up_out, up_send, up_recv, after, back_up_in)
    dn_args = (back_dn_out, dn_send, dn_recv, before, back_dn_in)

    def use_slice(place, last):
        x = rows_in[:, :features]
        gate_up, gate_dn = split(jnp.dot(x, wg[place], preferred_element_type=F32))
        upper_up, upper_dn = split(jnp.dot(x, wu[place], preferred_element_type=F32))
        middle = (jax.nn.silu(gate_up) * upper_up).astype(BF16)

        def add_up(step, _):
            at = pl.ds(pl.multiple_of(step * width, width), width)
            acc_up[:, at] += jnp.dot(middle, wd[place, :, at], preferred_element_type=F32)
            return 0

        lax.fori_loop(0, features // width, add_up, 0)
        if last:
            send_back(acc_up, *up_args)

        g_rows = rows_in[:, features:]
        low, _ = split(contract_last(g_rows, wd[place, :, :half]))
        _, high = split(contract_last(g_rows, wd[place, :, half:]))
        pulled = low + high
        sigma = jax.nn.sigmoid(gate_dn)
        d_gate = (pulled * upper_dn * sigma * (1.0 + gate_dn * (1.0 - sigma))).astype(BF16)
        d_upper = (pulled * gate_dn * sigma).astype(BF16)

        def add_dn(step, _):
            at = pl.ds(pl.multiple_of(step * width, width), width)
            acc_dn[:, at] += contract_last(d_gate, wg[place, at, :]) + contract_last(d_upper, wu[place, at, :])
            return 0

        lax.fori_loop(0, features // width, add_dn, 0)
        if last:
            send_back(acc_dn, *dn_args)

    forward(0)
    forward(1)
    forward(2)
    for slot in range(n_src):
        remote(
            row_block(rows_in, slot), row_block(rows_in, slot), row_send.at[slot], row_recv.at[slot], sec, sibling
        ).wait_recv()
    for place in range(3):
        wait_sibling(place)

    def early(place, _):
        use_slice(place, False)
        return 0

    lax.fori_loop(0, 3, early, 0)
    forward(3)
    wait_sibling(3)
    use_slice(3, True)

    for copy in residuals:
        copy.wait_recv()

    def unpick(route_row):
        lane = lax.broadcasted_iota(jnp.int32, (tokens, n_rows), 1).astype(F32)
        at = column(block_rows(route_row))
        return jnp.concatenate([lane == at, lane == at + float(CAP)], axis=0).astype(BF16)

    def wait_back(out, send, recv, section, into):
        for g in range(EXPERTS):
            remote(
                row_block(into, g), row_block(into, g), send.at[g], recv.at[g], section, me
            ).wait_recv()

    wait_back(*up_args)
    pick_up = unpick(meta_up_in[0:1, :])
    gate_up_col = column(meta_up_in[1:2, :])

    def finish_up(step, _):
        at = pl.ds(pl.multiple_of(step * width, width), width)
        back = jnp.dot(pick_up, back_up_in[:, at], preferred_element_type=F32)
        for h in range(2):
            to = pl.ds(pl.multiple_of(h * half + step * width, width), width)
            mixed = back[h * tokens:(h + 1) * tokens] * gate_up_col
            out_up[:, to] = (act_in[:, to].astype(F32) + mixed).astype(BF16)
        return 0

    lax.fori_loop(0, half // width, finish_up, 0)

    wait_back(*dn_args)
    pick_dn = unpick(meta_dn_in[2:3, :])
    gate_dn_col = column(meta_dn_in[3:4, :])

    def pull_dn(step, carry):
        squares, dots = carry
        at = pl.ds(pl.multiple_of(step * width, width), width)
        back = jnp.dot(pick_dn, back_dn_in[:, at], preferred_element_type=F32)
        for h in range(2):
            to = pl.ds(pl.multiple_of(h * half + step * width, width), width)
            u = back[h * tokens:(h + 1) * tokens] * gate_dn_col * gain_in[0:1, to]
            acc_dn[:tokens, to] = u
            x = saved_in[:, to].astype(F32)
            squares = squares + jnp.sum(x * x, axis=-1, keepdims=True)
            dots = dots + jnp.sum(x * u, axis=-1, keepdims=True)
        return squares, dots

    zero = jnp.zeros((tokens, 1), F32)
    squares, dots = lax.fori_loop(0, half // width, pull_dn, (zero, zero))
    r = lax.rsqrt(squares / features + EPS)
    pull = r * r * r * (dots / features)

    def finish_dn(step, _):
        to = pl.ds(pl.multiple_of(step * width, width), width)
        x = saved_in[:, to].astype(F32)
        out_dn[:, to] = (grad_in[:, to].astype(F32) + r * acc_dn[:tokens, to] - x * pull).astype(BF16)
        return 0

    lax.fori_loop(0, features // width, finish_dn, 0)

    for index in range(3):
        for h in range(2):

            @pl.when(jnp.logical_not(jnp.logical_and(own_host == z, c == h)))
            def _():
                slice_copy(index, h).wait_send()

    for g in range(EXPERTS):
        peer, copy = row_copy(g)

        @pl.when(peer != me)
        def _():
            copy.wait_send()

    for copy in residuals:
        copy.wait_send()
    for place in range(4):
        for index in range(3):
            sibling_copy(place, index).wait_send()

            @pl.when(leads_at(place))
            def _():
                host_copy(place, index).wait_send()

    for q in range(n_src):
        back_copy(q, *up_args).wait_send()
        back_copy(q, *dn_args).wait_send()


def per_device(
    act_up, routes_up, gates_up, saved_down, grad_down, routes_down, gates_down, norm_gain, w_gate, w_up, w_down,
):
    tokens, features = act_up.shape[1:]
    hidden = w_gate.shape[3]
    half = features // 2
    rows = EXPERTS * BLOCK
    meta = jnp.concatenate(
        [
            routes_up.reshape(1, tokens).astype(F32),
            gates_up.reshape(1, tokens),
            routes_down.reshape(1, tokens).astype(F32),
            gates_down.reshape(1, tokens),
            jnp.zeros((4, tokens), F32),
        ],
        axis=0,
    )
    vmem = pl.BlockSpec(memory_space=pltpu.VMEM)
    hbm = pl.BlockSpec(memory_space=pl.ANY)
    dma = pltpu.SemaphoreType.DMA
    up, down = pl.pallas_call(
        kernel,
        out_shape=(jax.ShapeDtypeStruct((tokens, features), BF16),) * 2,
        in_specs=[vmem] * 5 + [hbm] * 3,
        out_specs=(vmem, vmem),
        scratch_shapes=[
            pltpu.VMEM((SLICES, features, hidden), BF16),
            pltpu.VMEM((SLICES, features, hidden), BF16),
            pltpu.VMEM((SLICES, hidden, features), BF16),
            pltpu.VMEM((2 * tokens, features + half), BF16),
            pltpu.VMEM((rows, features + half), BF16),
            pltpu.VMEM((rows, features + half), BF16),
            pltpu.VMEM((EXPERTS * CAP, features), F32),
            pltpu.VMEM((EXPERTS * CAP, features), F32),
            pltpu.VMEM((rows, half), BF16),
            pltpu.VMEM((rows, half), BF16),
            pltpu.VMEM((rows, half), BF16),
            pltpu.VMEM((rows, half), BF16),
            pltpu.VMEM((tokens, features), BF16),
            pltpu.VMEM((tokens, features), BF16),
            pltpu.VMEM((tokens, features), BF16),
            pltpu.VMEM((1, features), F32),
            pltpu.VMEM((8, tokens), F32),
            pltpu.VMEM((8, tokens), F32),
            dma((EXPERTS,)),
            dma((EXPERTS,)),
            dma((3, 2)),
            dma((SLICES, 3, 2)),
            dma((SLICES, 3)),
            dma((SLICES, 3)),
            dma((EXPERTS,)),
            dma((EXPERTS,)),
            dma((EXPERTS,)),
            dma((EXPERTS,)),
            dma((6,)),
            dma((6,)),
        ],
        compiler_params=pltpu.CompilerParams(
            collective_id=0, has_side_effects=True, vmem_limit_bytes=60 * MIB
        ),
        cost_estimate=pl.CostEstimate(flops=12_000_000_000, bytes_accessed=12_000_000, transcendentals=400_000),
    )(
        act_up[0], saved_down[0], grad_down[0], norm_gain, meta, w_gate[0, 0], w_up[0, 0], w_down[0, 0],
    )
    return up[None], down[None]


def solution(mesh):
    tokens = P("section", "expert", None)
    weights = P("section", "expert", None, None)
    return jax.shard_map(
        per_device,
        mesh=mesh,
        in_specs=(tokens,) * 7 + (P("section", None),) + (weights,) * 3,
        out_specs=(tokens, tokens),
        check_vma=False,
    )
```

```python
import functools

import jax
import jax.numpy as jnp
from jax import lax
from jax.experimental import pallas as pl
from jax.experimental.pallas import tpu as pltpu
from jax.sharding import PartitionSpec as P

EPS = 1e-06
CAP = 24
BLOCK = 2 * CAP
EXPERTS = 8
SLICES = 4
MIB = 1024 * 1024
MESH = pl.DeviceIdType.MESH
F32 = jnp.float32
BF16 = jnp.bfloat16


def nearest(rel):
    inside = lax.rem(rel + 7, 8) // 4
    second = 1 - inside
    dist = second * (rel - 1) + inside * lax.rem(8 - rel, 8)
    return second, dist


def expert_home(zl, yh, c):
    return zl * 4 + yh * 2 + c


def column(row):
    n = row.shape[1]
    eye = lax.broadcasted_iota(jnp.int32, (n, n), 0) == lax.broadcasted_iota(jnp.int32, (n, n), 1)
    return jnp.sum(jnp.where(eye, row, 0.0), axis=1, keepdims=True)


def block_rows(route_row):
    n = route_row.shape[1]
    earlier = lax.broadcasted_iota(jnp.int32, (n, n), 0) < lax.broadcasted_iota(jnp.int32, (n, n), 1)
    same = jnp.logical_and(column(route_row) == route_row, earlier)
    slot = jnp.sum(jnp.where(same, 1.0, 0.0), axis=0, keepdims=True)
    return route_row * float(BLOCK) + slot


def contract_last(a, b):
    return lax.dot_general(a, b, (((1,), (1,)), ((), ())), preferred_element_type=F32)


def kernel(
    act, saved, grad, gain, meta, wg_in, wu_in, wd_in,
    out_up, out_dn,
    wg, wu, wd, table, packed, rows_in, acc_up, acc_dn,
    back_up_out, back_dn_out, back_up_in, back_dn_in,
    act_in, saved_in, grad_in, gain_in, meta_up_in, meta_dn_in,
    row_send, row_recv, src_send, w_recv, sib_send, fwd_send,
    up_send, up_recv, dn_send, dn_recv, res_send, res_recv,
):
    tokens, features = act.shape
    half = features // 2
    hidden = wg_in.shape[1]
    n_sec = lax.axis_size("section")
    sec = lax.axis_index("section")
    me = lax.axis_index("expert")
    z, yh, c = me // 4, lax.rem(me // 2, 2), lax.rem(me, 2)
    after = lax.rem(sec + 1, n_sec)
    before = lax.rem(sec + n_sec - 1, n_sec)

    own_zl = lax.rem(z, 2)
    own_first = 2 * (2 * c + own_zl)
    own_rel = lax.rem(z - own_first + 8, 8)
    own_second, _ = nearest(own_rel)
    own_host = own_first + own_second
    m = own_rel // 2
    own_place = (1 - own_zl) * (m + m // 2 - 2 * (m // 3)) + own_zl * (2 * m - m // 2 - 4 * (m // 3))

    pair = z // 2
    side = lax.rem(z, 2)
    host_zl, host_c = lax.rem(pair, 2), pair // 2
    host_expert = expert_home(host_zl, yh, host_c)
    other_host = (2 * pair + 1 - side) * 4 + yh * 2 + c
    sibling = z * 4 + yh * 2 + 1 - c
    leads_even = 1 - lax.rem(host_zl + side, 2)

    def source(dist, src_yh):
        src_z = lax.rem(2 * pair + side + (2 * side - 1) * dist + 8, 8)
        return src_z * 4 + src_yh * 2 + c

    def host_of(g):
        zl, g_yh, g_c = g // 4, (g // 2) % 2, g % 2
        first = 2 * (2 * g_c + zl)
        second, dist = nearest(lax.rem(z - first + 8, 8))
        return (first + second) * 4 + g_yh * 2 + c, dist * 2 + yh

    def slice_source(place):
        rel = (1 - host_zl) * (0, 2, 6, 4)[place] + host_zl * (1, 7, 3, 5)[place]
        return lax.rem(2 * pair + rel, 8) * 4 + yh * 2 + host_c

    barrier = pltpu.get_barrier_semaphore()

    def greet(section, peer):
        pl.semaphore_signal(barrier, inc=1, device_id=(section, peer), device_id_type=MESH)

    for dist in range(4):
        for src_yh in range(2):
            peer = source(dist, src_yh)

            @pl.when(peer != me)
            def _():
                greet(sec, peer)

    for place in range(4):
        peer = slice_source(place)
        leads = leads_even if place % 2 == 0 else 1 - leads_even

        @pl.when(jnp.logical_and(leads == 1, peer != me))
        def _():
            greet(sec, peer)

    greet(sec, other_host)
    greet(sec, sibling)
    for g in range(EXPERTS):
        peer, _ = host_of(g)
        greet(before, peer)
        greet(after, peer)
    greet(before, me)
    greet(after, me)
    here = jnp.where(own_host == z, 1, 0)
    pl.semaphore_wait(barrier, 29 - here)

    mats = ((wg_in, wg), (wu_in, wu), (wd_in, wd))

    def w_half(ref, index, h):
        size = mats[index][0].shape[0] // 2
        return ref.at[pl.ds(pl.multiple_of(h * size, 128), size)]

    def remote(src, dst, send, recv, section, peer):
        return pltpu.make_async_remote_copy(
            src_ref=src, dst_ref=dst, send_sem=send, recv_sem=recv,
            device_id=(section, peer), device_id_type=MESH,
        )

    def slice_copy(index, h):
        src, dst = mats[index]
        return remote(
            w_half(src, index, h), w_half(dst.at[own_place], index, h),
            src_send.at[index, h], w_recv.at[own_place, index, h], sec, own_host * 4 + yh * 2 + h,
        )

    for index in range(3):
        for h in range(2):
            mine = jnp.logical_and(own_host == z, c == h)

            @pl.when(mine)
            def _():
                src, dst = mats[index]
                pltpu.make_async_copy(
                    w_half(src, index, h), w_half(dst.at[own_place], index, h), w_recv.at[own_place, index, h]
                ).start()

            @pl.when(jnp.logical_not(mine))
            def _():
                slice_copy(index, h).start()

    gain_row = gain[...]
    rows_step = 16

    def norm_rows(step, _):
        at = pl.ds(pl.multiple_of(step * rows_step, rows_step), rows_step)
        for source_ref, base in ((act, 0), (saved, tokens)):
            values = source_ref[at, :].astype(F32)
            scaling = lax.rsqrt(jnp.mean(values * values, axis=-1, keepdims=True) + EPS)
            to = pl.ds(pl.multiple_of(base + step * rows_step, rows_step), rows_step)
            table[to, :features] = (values * scaling * gain_row).astype(BF16)
        return 0

    lax.fori_loop(0, tokens // rows_step, norm_rows, 0)
    table[:tokens, features:] = grad[:, :half]
    table[tokens:, features:] = grad[:, half:]

    at_up = block_rows(meta[0:1, :])
    at_dn = block_rows(meta[2:3, :])
    n_rows = EXPERTS * BLOCK
    row_index = lax.broadcasted_iota(jnp.int32, (n_rows, 2 * tokens), 0).astype(F32)
    pick_h = (row_index == jnp.concatenate([at_up, at_dn + float(CAP)], axis=1)).astype(BF16)
    pick_g = (row_index == jnp.concatenate([at_dn, at_dn + float(CAP)], axis=1)).astype(BF16)
    width = 256

    def pack(first, pick):
        def body(step, _):
            at = pl.ds(pl.multiple_of(first + step * width, width), width)
            packed[:, at] = jnp.dot(pick, table[:, at], preferred_element_type=F32).astype(BF16)
            return 0

        return body

    lax.fori_loop(0, features // width, pack(0, pick_h), 0)
    lax.fori_loop(0, half // width, pack(features, pick_g), 0)

    def row_block(ref, index):
        return ref.at[pl.ds(pl.multiple_of(index * BLOCK, BLOCK), BLOCK)]

    def row_copy(g):
        peer, slot = host_of(g)
        return peer, remote(
            row_block(packed, g), row_block(rows_in, slot), row_send.at[g], row_recv.at[slot], sec, peer
        )

    for g in range(EXPERTS):
        peer, slot = host_of(g)

        @pl.when(peer == me)
        def _():
            pltpu.make_async_copy(row_block(packed, g), row_block(rows_in, slot), row_recv.at[slot]).start()

        @pl.when(peer != me)
        def _():
            row_copy(g)[1].start()

    residuals = [
        remote(act, act_in, res_send.at[0], res_recv.at[0], after, me),
        remote(meta, meta_up_in, res_send.at[1], res_recv.at[1], after, me),
        remote(saved, saved_in, res_send.at[2], res_recv.at[2], before, me),
        remote(grad, grad_in, res_send.at[3], res_recv.at[3], before, me),
        remote(gain, gain_in, res_send.at[4], res_recv.at[4], before, me),
        remote(meta, meta_dn_in, res_send.at[5], res_recv.at[5], before, me),
    ]

    acc_up[...] = jnp.zeros_like(acc_up)
    acc_dn[...] = jnp.zeros_like(acc_dn)

    def half_copy(place, index, h, send, peer):
        view = w_half(mats[index][1].at[place], index, h)
        return remote(view, view, send, w_recv.at[place, index, h], sec, peer)

    def sibling_copy(place, index):
        return half_copy(place, index, c, sib_send.at[place, index], sibling)

    def host_copy(n, index):
        return half_copy(lead_place(n), index, c, fwd_send.at[n, index], other_host)

    def lead_place(n):
        return 2 * n + 1 - leads_even

    def follow_place(n):
        return 2 * n + leads_even

    def lead(n):
        for index in range(3):
            sibling_copy(lead_place(n), index).wait_recv()
            host_copy(n, index).start()
            sibling_copy(lead_place(n), index).start()

    def follow(n):
        for index in range(3):
            sibling_copy(follow_place(n), index).wait_recv()
            sibling_copy(follow_place(n), index).start()

    def wait_sibling(place):
        for index in range(3):
            half_copy(place, index, 1 - c, sib_send.at[place, index], sibling).wait_recv()

    n_src = EXPERTS

    def split(stacked):
        blocks = stacked.reshape(n_src, BLOCK, hidden)
        return (
            blocks[:, :CAP].reshape(n_src * CAP, hidden),
            blocks[:, CAP:].reshape(n_src * CAP, hidden),
        )

    def send_back(acc, out, send, recv, section, into):
        for dist in (3, 2, 1, 0):
            for src_yh in range(2):
                q = dist * 2 + src_yh
                both = jnp.concatenate(
                    [acc[q * CAP:(q + 1) * CAP, :half], acc[q * CAP:(q + 1) * CAP, half:]], axis=0
                )
                out[q * BLOCK:(q + 1) * BLOCK, :] = both.astype(BF16)
                back_copy(q, out, send, recv, section, into).start()

    def back_copy(q, out, send, recv, section, into):
        return remote(
            row_block(out, q), row_block(into, host_expert), send.at[q], recv.at[host_expert],
            section, source(q // 2, q % 2),
        )

    up_args = (back_up_out, up_send, up_recv, after, back_up_in)
    dn_args = (back_dn_out, dn_send, dn_recv, before, back_dn_in)

    def use_slice(place, last):
        x = rows_in[:, :features]
        gate_up, gate_dn = split(jnp.dot(x, wg[place], preferred_element_type=F32))
        upper_up, upper_dn = split(jnp.dot(x, wu[place], preferred_element_type=F32))
        middle = (jax.nn.silu(gate_up) * upper_up).astype(BF16)

        def add_up(step, _):
            at = pl.ds(pl.multiple_of(step * width, width), width)
            acc_up[:, at] += jnp.dot(middle, wd[place, :, at], preferred_element_type=F32)
            return 0

        lax.fori_loop(0, features // width, add_up, 0)
        if last:
            send_back(acc_up, *up_args)

        g_rows = rows_in[:, features:]
        low, _ = split(contract_last(g_rows, wd[place, :, :half]))
        _, high = split(contract_last(g_rows, wd[place, :, half:]))
        pulled = low + high
        sigma = jax.nn.sigmoid(gate_dn)
        d_gate = (pulled * upper_dn * sigma * (1.0 + gate_dn * (1.0 - sigma))).astype(BF16)
        d_upper = (pulled * gate_dn * sigma).astype(BF16)

        def add_dn(step, _):
            at = pl.ds(pl.multiple_of(step * width, width), width)
            acc_dn[:, at] += contract_last(d_gate, wg[place, at, :]) + contract_last(d_upper, wu[place, at, :])
            return 0

        lax.fori_loop(0, features // width, add_dn, 0)
        if last:
            send_back(acc_dn, *dn_args)

    lead(0)
    lead(1)
    follow(0)
    for copy in residuals:
        copy.start()

    for slot in range(n_src):
        remote(
            row_block(rows_in, slot), row_block(rows_in, slot), row_send.at[slot], row_recv.at[slot], sec, sibling
        ).wait_recv()
    for place in (lead_place(0), lead_place(1), follow_place(0)):
        wait_sibling(place)

    def early(step, _):
        use_slice((step // 2) * lead_place(1) + (1 - step // 2) * (lead_place(0) + lax.rem(step, 2) * (2 * leads_even - 1)), False)
        return 0

    lax.fori_loop(0, 3, early, 0)
    follow(1)
    wait_sibling(follow_place(1))
    use_slice(follow_place(1), True)

    for copy in residuals:
        copy.wait_recv()

    def unpick(route_row):
        lane = lax.broadcasted_iota(jnp.int32, (tokens, n_rows), 1).astype(F32)
        at = column(block_rows(route_row))
        return jnp.concatenate([lane == at, lane == at + float(CAP)], axis=0).astype(BF16)

    def wait_back(out, send, recv, section, into):
        for g in range(EXPERTS):
            remote(
                row_block(into, g), row_block(into, g), send.at[g], recv.at[g], section, me
            ).wait_recv()

    wait_back(*up_args)
    pick_up = unpick(meta_up_in[0:1, :])
    gate_up_col = column(meta_up_in[1:2, :])

    def finish_up(step, _):
        at = pl.ds(pl.multiple_of(step * width, width), width)
        back = jnp.dot(pick_up, back_up_in[:, at], preferred_element_type=F32)
        for h in range(2):
            to = pl.ds(pl.multiple_of(h * half + step * width, width), width)
            mixed = back[h * tokens:(h + 1) * tokens] * gate_up_col
            out_up[:, to] = (act_in[:, to].astype(F32) + mixed).astype(BF16)
        return 0

    lax.fori_loop(0, half // width, finish_up, 0)

    wait_back(*dn_args)
    pick_dn = unpick(meta_dn_in[2:3, :])
    gate_dn_col = column(meta_dn_in[3:4, :])

    def pull_dn(step, carry):
        squares, dots = carry
        at = pl.ds(pl.multiple_of(step * width, width), width)
        back = jnp.dot(pick_dn, back_dn_in[:, at], preferred_element_type=F32)
        for h in range(2):
            to = pl.ds(pl.multiple_of(h * half + step * width, width), width)
            u = back[h * tokens:(h + 1) * tokens] * gate_dn_col * gain_in[0:1, to]
            acc_dn[:tokens, to] = u
            x = saved_in[:, to].astype(F32)
            squares = squares + jnp.sum(x * x, axis=-1, keepdims=True)
            dots = dots + jnp.sum(x * u, axis=-1, keepdims=True)
        return squares, dots

    zero = jnp.zeros((tokens, 1), F32)
    squares, dots = lax.fori_loop(0, half // width, pull_dn, (zero, zero))
    r = lax.rsqrt(squares / features + EPS)
    pull = r * r * r * (dots / features)

    def finish_dn(step, _):
        to = pl.ds(pl.multiple_of(step * width, width), width)
        x = saved_in[:, to].astype(F32)
        out_dn[:, to] = (grad_in[:, to].astype(F32) + r * acc_dn[:tokens, to] - x * pull).astype(BF16)
        return 0

    lax.fori_loop(0, features // width, finish_dn, 0)

    for index in range(3):
        for h in range(2):

            @pl.when(jnp.logical_not(jnp.logical_and(own_host == z, c == h)))
            def _():
                slice_copy(index, h).wait_send()

    for g in range(EXPERTS):
        peer, copy = row_copy(g)

        @pl.when(peer != me)
        def _():
            copy.wait_send()

    for copy in residuals:
        copy.wait_send()
    for place in range(4):
        for index in range(3):
            sibling_copy(place, index).wait_send()
    for n in range(2):
        for index in range(3):
            host_copy(n, index).wait_send()
    for q in range(n_src):
        back_copy(q, *up_args).wait_send()
        back_copy(q, *dn_args).wait_send()


def per_device(
    act_up, routes_up, gates_up, saved_down, grad_down, routes_down, gates_down, norm_gain, w_gate, w_up, w_down,
):
    tokens, features = act_up.shape[1:]
    hidden = w_gate.shape[3]
    half = features // 2
    rows = EXPERTS * BLOCK
    meta = jnp.concatenate(
        [
            routes_up.reshape(1, tokens).astype(F32),
            gates_up.reshape(1, tokens),
            routes_down.reshape(1, tokens).astype(F32),
            gates_down.reshape(1, tokens),
            jnp.zeros((4, tokens), F32),
        ],
        axis=0,
    )
    vmem = pl.BlockSpec(memory_space=pltpu.VMEM)
    hbm = pl.BlockSpec(memory_space=pl.ANY)
    dma = pltpu.SemaphoreType.DMA
    up, down = pl.pallas_call(
        kernel,
        out_shape=(jax.ShapeDtypeStruct((tokens, features), BF16),) * 2,
        in_specs=[vmem] * 5 + [hbm] * 3,
        out_specs=(vmem, vmem),
        scratch_shapes=[
            pltpu.VMEM((SLICES, features, hidden), BF16),
            pltpu.VMEM((SLICES, features, hidden), BF16),
            pltpu.VMEM((SLICES, hidden, features), BF16),
            pltpu.VMEM((2 * tokens, features + half), BF16),
            pltpu.VMEM((rows, features + half), BF16),
            pltpu.VMEM((rows, features + half), BF16),
            pltpu.VMEM((EXPERTS * CAP, features), F32),
            pltpu.VMEM((EXPERTS * CAP, features), F32),
            pltpu.VMEM((rows, half), BF16),
            pltpu.VMEM((rows, half), BF16),
            pltpu.VMEM((rows, half), BF16),
            pltpu.VMEM((rows, half), BF16),
            pltpu.VMEM((tokens, features), BF16),
            pltpu.VMEM((tokens, features), BF16),
            pltpu.VMEM((tokens, features), BF16),
            pltpu.VMEM((1, features), F32),
            pltpu.VMEM((8, tokens), F32),
            pltpu.VMEM((8, tokens), F32),
            dma((EXPERTS,)),
            dma((EXPERTS,)),
            dma((3, 2)),
            dma((SLICES, 3, 2)),
            dma((SLICES, 3)),
            dma((2, 3)),
            dma((EXPERTS,)),
            dma((EXPERTS,)),
            dma((EXPERTS,)),
            dma((EXPERTS,)),
            dma((6,)),
            dma((6,)),
        ],
        compiler_params=pltpu.CompilerParams(
            collective_id=0, has_side_effects=True, vmem_limit_bytes=60 * MIB
        ),
        cost_estimate=pl.CostEstimate(flops=12_000_000_000, bytes_accessed=12_000_000, transcendentals=400_000),
    )(
        act_up[0], saved_down[0], grad_down[0], norm_gain, meta, w_gate[0, 0], w_up[0, 0], w_down[0, 0],
    )
    return up[None], down[None]


def solution(mesh):
    tokens = P("section", "expert", None)
    weights = P("section", "expert", None, None)
    return jax.shard_map(
        per_device,
        mesh=mesh,
        in_specs=(tokens,) * 7 + (P("section", None),) + (weights,) * 3,
        out_specs=(tokens, tokens),
        check_vma=False,
    )
```

```python
import functools

import jax
import jax.numpy as jnp
from jax import lax
from jax.experimental import pallas as pl
from jax.experimental.pallas import tpu as pltpu
from jax.sharding import PartitionSpec as P

EPS = 1e-06
CAP = 24
BLOCK = 2 * CAP
EXPERTS = 8
SLICES = 4
MIB = 1024 * 1024
MESH = pl.DeviceIdType.MESH
F32 = jnp.float32
BF16 = jnp.bfloat16


def nearest(rel):
    inside = lax.rem(rel + 7, 8) // 4
    second = 1 - inside
    dist = second * (rel - 1) + inside * lax.rem(8 - rel, 8)
    return second, dist


def expert_home(zl, yh, c):
    return zl * 4 + yh * 2 + c


def column(row):
    n = row.shape[1]
    eye = lax.broadcasted_iota(jnp.int32, (n, n), 0) == lax.broadcasted_iota(jnp.int32, (n, n), 1)
    return jnp.sum(jnp.where(eye, row, 0.0), axis=1, keepdims=True)


def block_rows(route_row):
    n = route_row.shape[1]
    earlier = lax.broadcasted_iota(jnp.int32, (n, n), 0) < lax.broadcasted_iota(jnp.int32, (n, n), 1)
    same = jnp.logical_and(column(route_row) == route_row, earlier)
    slot = jnp.sum(jnp.where(same, 1.0, 0.0), axis=0, keepdims=True)
    return route_row * float(BLOCK) + slot


def contract_last(a, b):
    return lax.dot_general(a, b, (((1,), (1,)), ((), ())), preferred_element_type=F32)


def kernel(
    act, saved, grad, gain, meta, wg_in, wu_in, wd_in,
    out_up, out_dn,
    wg, wu, wd, table_up, table_dn, packed_up, packed_dn, rows_up, rows_dn, x_up, x_dn, g_dn, acc_up, acc_dn,
    back_up_out, back_dn_out, back_up_in, back_dn_in,
    act_in, saved_in, grad_in, gain_in, meta_up_in, meta_dn_in,
    row_send, row_recv, src_send, w_recv, sib_send, fwd_send,
    up_send, up_recv, dn_send, dn_recv, res_send, res_recv,
):
    tokens, features = act.shape
    half = features // 2
    hidden = wg_in.shape[1]
    n_sec = lax.axis_size("section")
    sec = lax.axis_index("section")
    me = lax.axis_index("expert")
    z, yh, c = me // 4, lax.rem(me // 2, 2), lax.rem(me, 2)
    after = lax.rem(sec + 1, n_sec)
    before = lax.rem(sec + n_sec - 1, n_sec)

    own_zl = lax.rem(z, 2)
    own_first = 2 * (2 * c + own_zl)
    own_rel = lax.rem(z - own_first + 8, 8)
    own_second, _ = nearest(own_rel)
    own_host = own_first + own_second
    m = own_rel // 2
    own_place = (1 - own_zl) * (m + m // 2 - 2 * (m // 3)) + own_zl * (2 * m - m // 2 - 4 * (m // 3))

    pair = z // 2
    side = lax.rem(z, 2)
    host_zl, host_c = lax.rem(pair, 2), pair // 2
    host_expert = expert_home(host_zl, yh, host_c)
    other_host = (2 * pair + 1 - side) * 4 + yh * 2 + c
    sibling = z * 4 + yh * 2 + 1 - c
    leads_even = 1 - lax.rem(host_zl + side, 2)

    def source(dist, src_yh):
        src_z = lax.rem(2 * pair + side + (2 * side - 1) * dist + 8, 8)
        return src_z * 4 + src_yh * 2 + c

    def host_of(g):
        zl, g_yh, g_c = g // 4, (g // 2) % 2, g % 2
        first = 2 * (2 * g_c + zl)
        second, dist = nearest(lax.rem(z - first + 8, 8))
        return (first + second) * 4 + g_yh * 2 + c, dist * 2 + yh

    def slice_source(place):
        rel = (1 - host_zl) * (0, 2, 6, 4)[place] + host_zl * (1, 7, 3, 5)[place]
        return lax.rem(2 * pair + rel, 8) * 4 + yh * 2 + host_c

    barrier = pltpu.get_barrier_semaphore()

    def greet(section, peer):
        pl.semaphore_signal(barrier, inc=1, device_id=(section, peer), device_id_type=MESH)

    for dist in range(4):
        for src_yh in range(2):
            peer = source(dist, src_yh)

            @pl.when(peer != me)
            def _():
                greet(sec, peer)

    for place in range(4):
        peer = slice_source(place)
        leads = leads_even if place % 2 == 0 else 1 - leads_even

        @pl.when(jnp.logical_and(leads == 1, peer != me))
        def _():
            greet(sec, peer)

    greet(sec, other_host)
    greet(sec, sibling)
    for g in range(EXPERTS):
        peer, _ = host_of(g)
        greet(before, peer)
        greet(after, peer)
    greet(before, me)
    greet(after, me)
    here = jnp.where(own_host == z, 1, 0)
    pl.semaphore_wait(barrier, 29 - here)

    mats = ((wg_in, wg), (wu_in, wu), (wd_in, wd))

    def w_half(ref, index, h):
        size = mats[index][0].shape[0] // 2
        return ref.at[pl.ds(pl.multiple_of(h * size, 128), size)]

    def remote(src, dst, send, recv, section, peer):
        return pltpu.make_async_remote_copy(
            src_ref=src, dst_ref=dst, send_sem=send, recv_sem=recv,
            device_id=(section, peer), device_id_type=MESH,
        )

    def slice_copy(index, h):
        src, dst = mats[index]
        return remote(
            w_half(src, index, h), w_half(dst.at[own_place], index, h),
            src_send.at[index, h], w_recv.at[own_place, index, h], sec, own_host * 4 + yh * 2 + h,
        )

    for index in range(3):
        for h in range(2):
            mine = jnp.logical_and(own_host == z, c == h)

            @pl.when(mine)
            def _():
                src, dst = mats[index]
                pltpu.make_async_copy(
                    w_half(src, index, h), w_half(dst.at[own_place], index, h), w_recv.at[own_place, index, h]
                ).start()

            @pl.when(jnp.logical_not(mine))
            def _():
                slice_copy(index, h).start()

    gain_row = gain[...]
    rows_step = 16

    def normed(ref, at):
        values = ref[at, :].astype(F32)
        scaling = lax.rsqrt(jnp.mean(values * values, axis=-1, keepdims=True) + EPS)
        return (values * scaling * gain_row).astype(BF16)

    def norm_up(step, _):
        at = pl.ds(pl.multiple_of(step * rows_step, rows_step), rows_step)
        to = pl.ds(pl.multiple_of(tokens + step * rows_step, rows_step), rows_step)
        rows = normed(act, at)
        table_up[at, :] = rows[:, :half]
        table_up[to, :] = rows[:, half:]
        return 0

    def norm_dn(step, _):
        at = pl.ds(pl.multiple_of(step * rows_step, rows_step), rows_step)
        table_dn[at, :] = normed(saved, at)
        return 0

    n_rows = EXPERTS * BLOCK
    width = 256

    def pack(route_row, table, packed):
        at = block_rows(route_row)
        row_index = lax.broadcasted_iota(jnp.int32, (n_rows, 2 * tokens), 0).astype(F32)
        pick = (row_index == jnp.concatenate([at, at + float(CAP)], axis=1)).astype(BF16)

        def body(step, _):
            at = pl.ds(pl.multiple_of(step * width, width), width)
            packed[:, at] = jnp.dot(pick, table[:, at], preferred_element_type=F32).astype(BF16)
            return 0

        lax.fori_loop(0, packed.shape[1] // width, body, 0)

    def row_block(ref, index):
        return ref.at[pl.ds(pl.multiple_of(index * BLOCK, BLOCK), BLOCK)]

    kinds = ((packed_up, rows_up), (packed_dn, rows_dn))

    def row_copy(kind, g):
        packed, rows = kinds[kind]
        peer, slot = host_of(g)
        return peer, remote(
            row_block(packed, g), row_block(rows, slot), row_send.at[kind, g], row_recv.at[kind, slot], sec, peer
        )

    def send_rows(kind):
        packed, rows = kinds[kind]
        for g in range(EXPERTS):
            peer, slot = host_of(g)

            @pl.when(peer == me)
            def _():
                pltpu.make_async_copy(
                    row_block(packed, g), row_block(rows, slot), row_recv.at[kind, slot]
                ).start()

            @pl.when(peer != me)
            def _():
                row_copy(kind, g)[1].start()

    def wait_rows(kind):
        rows = kinds[kind][1]
        for slot in range(EXPERTS):
            view = row_block(rows, slot)
            remote(view, view, row_send.at[kind, slot], row_recv.at[kind, slot], sec, sibling).wait_recv()

    lax.fori_loop(0, tokens // rows_step, norm_up, 0)
    pack(meta[0:1, :], table_up, packed_up)
    send_rows(0)
    lax.fori_loop(0, tokens // rows_step, norm_dn, 0)
    table_dn[tokens:, :] = grad[...]
    pack(meta[2:3, :], table_dn, packed_dn)

    residuals = [
        remote(act, act_in, res_send.at[0], res_recv.at[0], after, me),
        remote(meta, meta_up_in, res_send.at[1], res_recv.at[1], after, me),
        remote(saved, saved_in, res_send.at[2], res_recv.at[2], before, me),
        remote(grad, grad_in, res_send.at[3], res_recv.at[3], before, me),
        remote(gain, gain_in, res_send.at[4], res_recv.at[4], before, me),
        remote(meta, meta_dn_in, res_send.at[5], res_recv.at[5], before, me),
    ]

    acc_up[...] = jnp.zeros_like(acc_up)
    acc_dn[...] = jnp.zeros_like(acc_dn)

    def half_copy(place, index, h, send, peer):
        view = w_half(mats[index][1].at[place], index, h)
        return remote(view, view, send, w_recv.at[place, index, h], sec, peer)

    def sibling_copy(place, index):
        return half_copy(place, index, c, sib_send.at[place, index], sibling)

    def host_copy(n, index):
        return half_copy(lead_place(n), index, c, fwd_send.at[n, index], other_host)

    def lead_place(n):
        return 2 * n + 1 - leads_even

    def follow_place(n):
        return 2 * n + leads_even

    def lead(n):
        for index in range(3):
            sibling_copy(lead_place(n), index).wait_recv()
            host_copy(n, index).start()
            sibling_copy(lead_place(n), index).start()

    def follow(n):
        for index in range(3):
            sibling_copy(follow_place(n), index).wait_recv()
            sibling_copy(follow_place(n), index).start()

    def wait_sibling(place):
        for index in range(3):
            half_copy(place, index, 1 - c, sib_send.at[place, index], sibling).wait_recv()

    n_src = EXPERTS

    def arrange(rows, low, high):
        def body(step, _):
            top = rows[pl.ds(pl.multiple_of(step * 2 * BLOCK, 2 * BLOCK), BLOCK), :].astype(F32)
            bottom = rows[pl.ds(pl.multiple_of((step * 2 + 1) * BLOCK, BLOCK), BLOCK), :].astype(F32)
            at = pl.ds(pl.multiple_of(step * BLOCK, BLOCK), BLOCK)
            low[at, :rows.shape[1]] = jnp.concatenate([top[:CAP], bottom[:CAP]], axis=0).astype(BF16)
            second = jnp.concatenate([top[CAP:], bottom[CAP:]], axis=0).astype(BF16)
            if high is None:
                low[at, rows.shape[1]:] = second
            else:
                high[at, :] = second
            return 0

        lax.fori_loop(0, n_src // 2, body, 0)

    def send_back(acc, out, send, recv, section, into):
        for dist in (3, 2, 1, 0):
            for src_yh in range(2):
                q = dist * 2 + src_yh
                both = jnp.concatenate(
                    [acc[q * CAP:(q + 1) * CAP, :half], acc[q * CAP:(q + 1) * CAP, half:]], axis=0
                )
                out[q * BLOCK:(q + 1) * BLOCK, :] = both.astype(BF16)
                back_copy(q, out, send, recv, section, into).start()

    def back_copy(q, out, send, recv, section, into):
        return remote(
            row_block(out, q), row_block(into, host_expert), send.at[q], recv.at[host_expert],
            section, source(q // 2, q % 2),
        )

    up_args = (back_up_out, up_send, up_recv, after, back_up_in)
    dn_args = (back_dn_out, dn_send, dn_recv, before, back_dn_in)

    def use_up(place):
        x = x_up[...]
        gate = jnp.dot(x, wg[place], preferred_element_type=F32)
        upper = jnp.dot(x, wu[place], preferred_element_type=F32)
        middle = (jax.nn.silu(gate) * upper).astype(BF16)

        def add_up(step, _):
            at = pl.ds(pl.multiple_of(step * width, width), width)
            acc_up[:, at] += jnp.dot(middle, wd[place, :, at], preferred_element_type=F32)
            return 0

        lax.fori_loop(0, features // width, add_up, 0)

    def use_dn(place):
        x = x_dn[...]
        gate = jnp.dot(x, wg[place], preferred_element_type=F32)
        upper = jnp.dot(x, wu[place], preferred_element_type=F32)
        pulled = contract_last(g_dn[...], wd[place])
        sigma = jax.nn.sigmoid(gate)
        d_gate = (pulled * upper * sigma * (1.0 + gate * (1.0 - sigma))).astype(BF16)
        d_upper = (pulled * gate * sigma).astype(BF16)

        def add_dn(step, _):
            at = pl.ds(pl.multiple_of(step * width, width), width)
            acc_dn[:, at] += contract_last(d_gate, wg[place, at, :]) + contract_last(d_upper, wu[place, at, :])
            return 0

        lax.fori_loop(0, features // width, add_dn, 0)

    def at_step(step):
        return 2 * (step // 2) + 1 - leads_even + lax.rem(step, 2) * (2 * leads_even - 1)

    def loop(use, first, end):
        def body(step, _):
            use(at_step(step))
            return 0

        lax.fori_loop(first, end, body, 0)

    lead(0)
    lead(1)
    send_rows(1)
    follow(0)
    for copy in residuals:
        copy.start()

    wait_rows(0)
    arrange(rows_up, x_up, None)
    for place in (lead_place(0), lead_place(1), follow_place(0)):
        wait_sibling(place)
    loop(use_up, 0, 3)
    follow(1)
    wait_sibling(follow_place(1))
    loop(use_up, 3, 4)
    send_back(acc_up, *up_args)
    wait_rows(1)
    arrange(rows_dn, x_dn, g_dn)
    loop(use_dn, 0, 4)
    send_back(acc_dn, *dn_args)

    for copy in residuals:
        copy.wait_recv()

    def unpick(route_row):
        lane = lax.broadcasted_iota(jnp.int32, (tokens, n_rows), 1).astype(F32)
        at = column(block_rows(route_row))
        return jnp.concatenate([lane == at, lane == at + float(CAP)], axis=0).astype(BF16)

    def wait_back(out, send, recv, section, into):
        for g in range(EXPERTS):
            remote(
                row_block(into, g), row_block(into, g), send.at[g], recv.at[g], section, me
            ).wait_recv()

    wait_back(*up_args)
    pick_up = unpick(meta_up_in[0:1, :])
    gate_up_col = column(meta_up_in[1:2, :])

    def finish_up(step, _):
        at = pl.ds(pl.multiple_of(step * width, width), width)
        back = jnp.dot(pick_up, back_up_in[:, at], preferred_element_type=F32)
        for h in range(2):
            to = pl.ds(pl.multiple_of(h * half + step * width, width), width)
            mixed = back[h * tokens:(h + 1) * tokens] * gate_up_col
            out_up[:, to] = (act_in[:, to].astype(F32) + mixed).astype(BF16)
        return 0

    lax.fori_loop(0, half // width, finish_up, 0)

    wait_back(*dn_args)
    pick_dn = unpick(meta_dn_in[2:3, :])
    gate_dn_col = column(meta_dn_in[3:4, :])

    def pull_dn(step, carry):
        squares, dots = carry
        at = pl.ds(pl.multiple_of(step * width, width), width)
        back = jnp.dot(pick_dn, back_dn_in[:, at], preferred_element_type=F32)
        for h in range(2):
            to = pl.ds(pl.multiple_of(h * half + step * width, width), width)
            u = back[h * tokens:(h + 1) * tokens] * gate_dn_col * gain_in[0:1, to]
            acc_dn[:tokens, to] = u
            x = saved_in[:, to].astype(F32)
            squares = squares + jnp.sum(x * x, axis=-1, keepdims=True)
            dots = dots + jnp.sum(x * u, axis=-1, keepdims=True)
        return squares, dots

    zero = jnp.zeros((tokens, 1), F32)
    squares, dots = lax.fori_loop(0, half // width, pull_dn, (zero, zero))
    r = lax.rsqrt(squares / features + EPS)
    pull = r * r * r * (dots / features)

    def finish_dn(step, _):
        to = pl.ds(pl.multiple_of(step * width, width), width)
        x = saved_in[:, to].astype(F32)
        out_dn[:, to] = (grad_in[:, to].astype(F32) + r * acc_dn[:tokens, to] - x * pull).astype(BF16)
        return 0

    lax.fori_loop(0, features // width, finish_dn, 0)

    for index in range(3):
        for h in range(2):

            @pl.when(jnp.logical_not(jnp.logical_and(own_host == z, c == h)))
            def _():
                slice_copy(index, h).wait_send()

    for kind in range(2):
        for g in range(EXPERTS):

            @pl.when(host_of(g)[0] != me)
            def _():
                row_copy(kind, g)[1].wait_send()

    for copy in residuals:
        copy.wait_send()
    for place in range(4):
        for index in range(3):
            sibling_copy(place, index).wait_send()
    for n in range(2):
        for index in range(3):
            host_copy(n, index).wait_send()
    for q in range(n_src):
        back_copy(q, *up_args).wait_send()
        back_copy(q, *dn_args).wait_send()


def per_device(
    act_up, routes_up, gates_up, saved_down, grad_down, routes_down, gates_down, norm_gain, w_gate, w_up, w_down,
):
    tokens, features = act_up.shape[1:]
    hidden = w_gate.shape[3]
    half = features // 2
    rows = EXPERTS * BLOCK
    meta = jnp.concatenate(
        [
            routes_up.reshape(1, tokens).astype(F32),
            gates_up.reshape(1, tokens),
            routes_down.reshape(1, tokens).astype(F32),
            gates_down.reshape(1, tokens),
            jnp.zeros((4, tokens), F32),
        ],
        axis=0,
    )
    vmem = pl.BlockSpec(memory_space=pltpu.VMEM)
    hbm = pl.BlockSpec(memory_space=pl.ANY)
    dma = pltpu.SemaphoreType.DMA
    up, down = pl.pallas_call(
        kernel,
        out_shape=(jax.ShapeDtypeStruct((tokens, features), BF16),) * 2,
        in_specs=[vmem] * 5 + [hbm] * 3,
        out_specs=(vmem, vmem),
        scratch_shapes=[
            pltpu.VMEM((SLICES, features, hidden), BF16),
            pltpu.VMEM((SLICES, features, hidden), BF16),
            pltpu.VMEM((SLICES, hidden, features), BF16),
            pltpu.VMEM((2 * tokens, half), BF16),
            pltpu.VMEM((2 * tokens, features), BF16),
            pltpu.VMEM((rows, half), BF16),
            pltpu.VMEM((rows, features), BF16),
            pltpu.VMEM((rows, half), BF16),
            pltpu.VMEM((rows, features), BF16),
            pltpu.VMEM((EXPERTS * CAP, features), BF16),
            pltpu.VMEM((EXPERTS * CAP, features), BF16),
            pltpu.VMEM((EXPERTS * CAP, features), BF16),
            pltpu.VMEM((EXPERTS * CAP, features), F32),
            pltpu.VMEM((EXPERTS * CAP, features), F32),
            pltpu.VMEM((rows, half), BF16),
            pltpu.VMEM((rows, half), BF16),
            pltpu.VMEM((rows, half), BF16),
            pltpu.VMEM((rows, half), BF16),
            pltpu.VMEM((tokens, features), BF16),
            pltpu.VMEM((tokens, features), BF16),
            pltpu.VMEM((tokens, features), BF16),
            pltpu.VMEM((1, features), F32),
            pltpu.VMEM((8, tokens), F32),
            pltpu.VMEM((8, tokens), F32),
            dma((2, EXPERTS)),
            dma((2, EXPERTS)),
            dma((3, 2)),
            dma((SLICES, 3, 2)),
            dma((SLICES, 3)),
            dma((2, 3)),
            dma((EXPERTS,)),
            dma((EXPERTS,)),
            dma((EXPERTS,)),
            dma((EXPERTS,)),
            dma((6,)),
            dma((6,)),
        ],
        compiler_params=pltpu.CompilerParams(
            collective_id=0, has_side_effects=True, vmem_limit_bytes=60 * MIB
        ),
        cost_estimate=pl.CostEstimate(flops=12_000_000_000, bytes_accessed=12_000_000, transcendentals=400_000),
    )(
        act_up[0], saved_down[0], grad_down[0], norm_gain, meta, w_gate[0, 0], w_up[0, 0], w_down[0, 0],
    )
    return up[None], down[None]


def solution(mesh):
    tokens = P("section", "expert", None)
    weights = P("section", "expert", None, None)
    return jax.shard_map(
        per_device,
        mesh=mesh,
        in_specs=(tokens,) * 7 + (P("section", None),) + (weights,) * 3,
        out_specs=(tokens, tokens),
        check_vma=False,
    )
```

```python
import functools

import jax
import jax.numpy as jnp
from jax import lax
from jax.experimental import pallas as pl
from jax.experimental.pallas import tpu as pltpu
from jax.sharding import PartitionSpec as P

EPS = 1e-06
CAP = 24
BLOCK = 2 * CAP
EXPERTS = 8
SLICES = 4
MIB = 1024 * 1024
MESH = pl.DeviceIdType.MESH
F32 = jnp.float32
BF16 = jnp.bfloat16


def nearest(rel):
    inside = lax.rem(rel + 7, 8) // 4
    second = 1 - inside
    dist = second * (rel - 1) + inside * lax.rem(8 - rel, 8)
    return second, dist


def expert_home(zl, yh, c):
    return zl * 4 + yh * 2 + c


def column(row):
    n = row.shape[1]
    eye = lax.broadcasted_iota(jnp.int32, (n, n), 0) == lax.broadcasted_iota(jnp.int32, (n, n), 1)
    return jnp.sum(jnp.where(eye, row, 0.0), axis=1, keepdims=True)


def block_rows(route_row):
    n = route_row.shape[1]
    earlier = lax.broadcasted_iota(jnp.int32, (n, n), 0) < lax.broadcasted_iota(jnp.int32, (n, n), 1)
    same = jnp.logical_and(column(route_row) == route_row, earlier)
    slot = jnp.sum(jnp.where(same, 1.0, 0.0), axis=0, keepdims=True)
    return route_row * float(BLOCK) + slot


def contract_last(a, b):
    return lax.dot_general(a, b, (((1,), (1,)), ((), ())), preferred_element_type=F32)


def kernel(
    act, saved, grad, gain, route_up, weight_up, route_dn, weight_dn, wg_in, wu_in, wd_in,
    out_up, out_dn,
    wg, wu, wd, table_up, table_dn, packed_up, packed_dn, rows_up, rows_dn, x_up, x_dn, g_dn, acc_up, acc_dn,
    back_up_out, back_dn_out, back_up_in, back_dn_in,
    act_in, saved_in, grad_in, gain_in, route_up_in, weight_up_in, route_dn_in, weight_dn_in,
    row_send, row_recv, src_send, w_recv, sib_send, fwd_send,
    up_send, up_recv, dn_send, dn_recv, res_send, res_recv,
):
    tokens, features = act.shape
    half = features // 2
    hidden = wg_in.shape[1]
    n_sec = lax.axis_size("section")
    sec = lax.axis_index("section")
    me = lax.axis_index("expert")
    z, yh, c = me // 4, lax.rem(me // 2, 2), lax.rem(me, 2)
    after = lax.rem(sec + 1, n_sec)
    before = lax.rem(sec + n_sec - 1, n_sec)

    own_zl = lax.rem(z, 2)
    own_first = 2 * (2 * c + own_zl)
    own_rel = lax.rem(z - own_first + 8, 8)
    own_second, _ = nearest(own_rel)
    own_host = own_first + own_second
    m = own_rel // 2
    own_place = (1 - own_zl) * (m + m // 2 - 2 * (m // 3)) + own_zl * (2 * m - m // 2 - 4 * (m // 3))

    pair = z // 2
    side = lax.rem(z, 2)
    host_zl, host_c = lax.rem(pair, 2), pair // 2
    host_expert = expert_home(host_zl, yh, host_c)
    other_host = (2 * pair + 1 - side) * 4 + yh * 2 + c
    sibling = z * 4 + yh * 2 + 1 - c
    leads_even = 1 - lax.rem(host_zl + side, 2)

    def source(dist, src_yh):
        src_z = lax.rem(2 * pair + side + (2 * side - 1) * dist + 8, 8)
        return src_z * 4 + src_yh * 2 + c

    def host_of(g):
        zl, g_yh, g_c = g // 4, (g // 2) % 2, g % 2
        first = 2 * (2 * g_c + zl)
        second, dist = nearest(lax.rem(z - first + 8, 8))
        return (first + second) * 4 + g_yh * 2 + c, dist * 2 + yh

    def slice_source(place):
        rel = (1 - host_zl) * (0, 2, 6, 4)[place] + host_zl * (1, 7, 3, 5)[place]
        return lax.rem(2 * pair + rel, 8) * 4 + yh * 2 + host_c

    barrier = pltpu.get_barrier_semaphore()

    def greet(section, peer):
        pl.semaphore_signal(barrier, inc=1, device_id=(section, peer), device_id_type=MESH)

    for dist in range(4):
        for src_yh in range(2):
            peer = source(dist, src_yh)

            @pl.when(peer != me)
            def _():
                greet(sec, peer)

    for place in range(4):
        peer = slice_source(place)
        leads = leads_even if place % 2 == 0 else 1 - leads_even

        @pl.when(jnp.logical_and(leads == 1, peer != me))
        def _():
            greet(sec, peer)

    greet(sec, other_host)
    greet(sec, sibling)
    greet(before, me)
    greet(after, me)
    mats = ((wg_in, wg), (wu_in, wu), (wd_in, wd))

    def w_half(ref, index, h):
        size = mats[index][0].shape[0] // 2
        return ref.at[pl.ds(pl.multiple_of(h * size, 128), size)]

    def remote(src, dst, send, recv, section, peer):
        return pltpu.make_async_remote_copy(
            src_ref=src, dst_ref=dst, send_sem=send, recv_sem=recv,
            device_id=(section, peer), device_id_type=MESH,
        )

    gain_row = gain[...]
    rows_step = 16

    def normed(ref, at):
        values = ref[at, :].astype(F32)
        scaling = lax.rsqrt(jnp.mean(values * values, axis=-1, keepdims=True) + EPS)
        return (values * scaling * gain_row).astype(BF16)

    def norm_up(step, _):
        at = pl.ds(pl.multiple_of(step * rows_step, rows_step), rows_step)
        to = pl.ds(pl.multiple_of(tokens + step * rows_step, rows_step), rows_step)
        rows = normed(act, at)
        table_up[at, :] = rows[:, :half]
        table_up[to, :] = rows[:, half:]
        return 0

    def norm_dn(step, _):
        at = pl.ds(pl.multiple_of(step * rows_step, rows_step), rows_step)
        table_dn[at, :] = normed(saved, at)
        return 0

    n_rows = EXPERTS * BLOCK
    width = 256

    def pack(route_row, table, packed):
        at = block_rows(route_row)
        row_index = lax.broadcasted_iota(jnp.int32, (n_rows, 2 * tokens), 0).astype(F32)
        pick = (row_index == jnp.concatenate([at, at + float(CAP)], axis=1)).astype(BF16)

        def body(step, _):
            at = pl.ds(pl.multiple_of(step * width, width), width)
            packed[:, at] = jnp.dot(pick, table[:, at], preferred_element_type=F32).astype(BF16)
            return 0

        lax.fori_loop(0, packed.shape[1] // width, body, 0)

    def row_block(ref, index):
        return ref.at[pl.ds(pl.multiple_of(index * BLOCK, BLOCK), BLOCK)]

    kinds = ((packed_up, rows_up), (packed_dn, rows_dn))

    def row_copy(kind, g):
        packed, rows = kinds[kind]
        peer, slot = host_of(g)
        return peer, remote(
            row_block(packed, g), row_block(rows, slot), row_send.at[kind, g], row_recv.at[kind, slot], sec, peer
        )

    def send_rows(kind):
        packed, rows = kinds[kind]
        for g in range(EXPERTS):
            peer, slot = host_of(g)

            @pl.when(peer == me)
            def _():
                pltpu.make_async_copy(
                    row_block(packed, g), row_block(rows, slot), row_recv.at[kind, slot]
                ).start()

            @pl.when(peer != me)
            def _():
                row_copy(kind, g)[1].start()

    def wait_rows(kind):
        rows = kinds[kind][1]
        for slot in range(EXPERTS):
            view = row_block(rows, slot)
            remote(view, view, row_send.at[kind, slot], row_recv.at[kind, slot], sec, sibling).wait_recv()

    lax.fori_loop(0, tokens // rows_step, norm_up, 0)
    pack(route_up[...].astype(F32), table_up, packed_up)
    here = jnp.where(own_host == z, 1, 0)
    pl.semaphore_wait(barrier, 13 - here)

    def slice_copy(index, h):
        src, dst = mats[index]
        return remote(
            w_half(src, index, h), w_half(dst.at[own_place], index, h),
            src_send.at[index, h], w_recv.at[own_place, index, h], sec, own_host * 4 + yh * 2 + h,
        )

    for index in range(3):
        for h in range(2):
            mine = jnp.logical_and(own_host == z, c == h)

            @pl.when(mine)
            def _():
                src, dst = mats[index]
                pltpu.make_async_copy(
                    w_half(src, index, h), w_half(dst.at[own_place], index, h), w_recv.at[own_place, index, h]
                ).start()

            @pl.when(jnp.logical_not(mine))
            def _():
                slice_copy(index, h).start()

    send_rows(0)
    lax.fori_loop(0, tokens // rows_step, norm_dn, 0)
    table_dn[tokens:, :] = grad[...]
    pack(route_dn[...].astype(F32), table_dn, packed_dn)

    residuals = [
        remote(act, act_in, res_send.at[0], res_recv.at[0], after, me),
        remote(route_up, route_up_in, res_send.at[1], res_recv.at[1], after, me),
        remote(weight_up, weight_up_in, res_send.at[6], res_recv.at[6], after, me),
        remote(saved, saved_in, res_send.at[2], res_recv.at[2], before, me),
        remote(grad, grad_in, res_send.at[3], res_recv.at[3], before, me),
        remote(gain, gain_in, res_send.at[4], res_recv.at[4], before, me),
        remote(route_dn, route_dn_in, res_send.at[5], res_recv.at[5], before, me),
        remote(weight_dn, weight_dn_in, res_send.at[7], res_recv.at[7], before, me),
    ]

    acc_up[...] = jnp.zeros_like(acc_up)
    acc_dn[...] = jnp.zeros_like(acc_dn)

    def half_copy(place, index, h, send, peer):
        view = w_half(mats[index][1].at[place], index, h)
        return remote(view, view, send, w_recv.at[place, index, h], sec, peer)

    def sibling_copy(place, index):
        return half_copy(place, index, c, sib_send.at[place, index], sibling)

    def host_copy(n, index):
        return half_copy(lead_place(n), index, c, fwd_send.at[n, index], other_host)

    def lead_place(n):
        return 2 * n + 1 - leads_even

    def follow_place(n):
        return 2 * n + leads_even

    def lead(n):
        for index in range(3):
            sibling_copy(lead_place(n), index).wait_recv()
            host_copy(n, index).start()
            sibling_copy(lead_place(n), index).start()

    def follow(n):
        for index in range(3):
            sibling_copy(follow_place(n), index).wait_recv()
            sibling_copy(follow_place(n), index).start()

    def wait_sibling(place):
        for index in range(3):
            half_copy(place, index, 1 - c, sib_send.at[place, index], sibling).wait_recv()

    n_src = EXPERTS

    def arrange(rows, low, high):
        def body(step, _):
            top = rows[pl.ds(pl.multiple_of(step * 2 * BLOCK, 2 * BLOCK), BLOCK), :].astype(F32)
            bottom = rows[pl.ds(pl.multiple_of((step * 2 + 1) * BLOCK, BLOCK), BLOCK), :].astype(F32)
            at = pl.ds(pl.multiple_of(step * BLOCK, BLOCK), BLOCK)
            low[at, :rows.shape[1]] = jnp.concatenate([top[:CAP], bottom[:CAP]], axis=0).astype(BF16)
            second = jnp.concatenate([top[CAP:], bottom[CAP:]], axis=0).astype(BF16)
            if high is None:
                low[at, rows.shape[1]:] = second
            else:
                high[at, :] = second
            return 0

        lax.fori_loop(0, n_src // 2, body, 0)

    def send_back(dists, acc, out, send, recv, section, into):
        for dist in dists:
            for src_yh in range(2):
                q = dist * 2 + src_yh
                both = jnp.concatenate(
                    [acc[q * CAP:(q + 1) * CAP, :half], acc[q * CAP:(q + 1) * CAP, half:]], axis=0
                )
                out[q * BLOCK:(q + 1) * BLOCK, :] = both.astype(BF16)
                back_copy(q, out, send, recv, section, into).start()

    def back_copy(q, out, send, recv, section, into):
        return remote(
            row_block(out, q), row_block(into, host_expert), send.at[q], recv.at[host_expert],
            section, source(q // 2, q % 2),
        )

    up_args = (back_up_out, up_send, up_recv, after, back_up_in)
    dn_args = (back_dn_out, dn_send, dn_recv, before, back_dn_in)

    def use_up(place, rows):
        x = x_up[rows, :]
        gate = jnp.dot(x, wg[place], preferred_element_type=F32)
        upper = jnp.dot(x, wu[place], preferred_element_type=F32)
        middle = (jax.nn.silu(gate) * upper).astype(BF16)

        def add_up(step, _):
            at = pl.ds(pl.multiple_of(step * width, width), width)
            acc_up[rows, at] += jnp.dot(middle, wd[place, :, at], preferred_element_type=F32)
            return 0

        lax.fori_loop(0, features // width, add_up, 0)

    def use_dn(place, rows):
        x = x_dn[rows, :]
        gate = jnp.dot(x, wg[place], preferred_element_type=F32)
        upper = jnp.dot(x, wu[place], preferred_element_type=F32)
        pulled = contract_last(g_dn[rows, :], wd[place])
        sigma = jax.nn.sigmoid(gate)
        d_gate = (pulled * upper * sigma * (1.0 + gate * (1.0 - sigma))).astype(BF16)
        d_upper = (pulled * gate * sigma).astype(BF16)

        def add_dn(step, _):
            at = pl.ds(pl.multiple_of(step * width, width), width)
            acc_dn[rows, at] += contract_last(d_gate, wg[place, at, :]) + contract_last(d_upper, wu[place, at, :])
            return 0

        lax.fori_loop(0, features // width, add_dn, 0)

    def at_step(step):
        return 2 * (step // 2) + 1 - leads_even + lax.rem(step, 2) * (2 * leads_even - 1)

    def loop(use, first, end, rows):
        def body(step, _):
            use(at_step(step), rows)
            return 0

        lax.fori_loop(first, end, body, 0)

    lead(0)
    lead(1)
    send_rows(1)
    follow(0)
    for copy in residuals:
        copy.start()

    wait_rows(0)
    arrange(rows_up, x_up, None)
    for place in (lead_place(0), lead_place(1), follow_place(0)):
        wait_sibling(place)
    part = n_src * CAP // 2
    near, far = pl.ds(0, part), pl.ds(part, part)
    loop(use_up, 0, 3, pl.ds(0, 2 * part))
    follow(1)
    wait_sibling(follow_place(1))
    loop(use_up, 3, 4, far)
    send_back((3, 2), acc_up, *up_args)
    loop(use_up, 3, 4, near)
    send_back((1, 0), acc_up, *up_args)
    wait_rows(1)
    arrange(rows_dn, x_dn, g_dn)
    loop(use_dn, 0, 4, far)
    send_back((3, 2), acc_dn, *dn_args)
    loop(use_dn, 0, 4, near)
    send_back((1, 0), acc_dn, *dn_args)

    for copy in residuals:
        copy.wait_recv()

    def unpick(route_row):
        lane = lax.broadcasted_iota(jnp.int32, (tokens, n_rows), 1).astype(F32)
        at = column(block_rows(route_row))
        return jnp.concatenate([lane == at, lane == at + float(CAP)], axis=0).astype(BF16)

    def wait_back(out, send, recv, section, into):
        for g in range(EXPERTS):
            remote(
                row_block(into, g), row_block(into, g), send.at[g], recv.at[g], section, me
            ).wait_recv()

    wait_back(*up_args)
    pick_up = unpick(route_up_in[...].astype(F32))
    gate_up_col = column(weight_up_in[...])

    def finish_up(step, _):
        at = pl.ds(pl.multiple_of(step * width, width), width)
        back = jnp.dot(pick_up, back_up_in[:, at], preferred_element_type=F32)
        for h in range(2):
            to = pl.ds(pl.multiple_of(h * half + step * width, width), width)
            mixed = back[h * tokens:(h + 1) * tokens] * gate_up_col
            out_up[:, to] = (act_in[:, to].astype(F32) + mixed).astype(BF16)
        return 0

    lax.fori_loop(0, half // width, finish_up, 0)

    wait_back(*dn_args)
    pick_dn = unpick(route_dn_in[...].astype(F32))
    gate_dn_col = column(weight_dn_in[...])

    def pull_dn(step, carry):
        squares, dots = carry
        at = pl.ds(pl.multiple_of(step * width, width), width)
        back = jnp.dot(pick_dn, back_dn_in[:, at], preferred_element_type=F32)
        for h in range(2):
            to = pl.ds(pl.multiple_of(h * half + step * width, width), width)
            u = back[h * tokens:(h + 1) * tokens] * gate_dn_col * gain_in[0:1, to]
            acc_dn[:tokens, to] = u
            x = saved_in[:, to].astype(F32)
            squares = squares + jnp.sum(x * x, axis=-1, keepdims=True)
            dots = dots + jnp.sum(x * u, axis=-1, keepdims=True)
        return squares, dots

    zero = jnp.zeros((tokens, 1), F32)
    squares, dots = lax.fori_loop(0, half // width, pull_dn, (zero, zero))
    r = lax.rsqrt(squares / features + EPS)
    pull = r * r * r * (dots / features)

    def finish_dn(step, _):
        to = pl.ds(pl.multiple_of(step * width, width), width)
        x = saved_in[:, to].astype(F32)
        out_dn[:, to] = (grad_in[:, to].astype(F32) + r * acc_dn[:tokens, to] - x * pull).astype(BF16)
        return 0

    lax.fori_loop(0, features // width, finish_dn, 0)

    for index in range(3):
        for h in range(2):

            @pl.when(jnp.logical_not(jnp.logical_and(own_host == z, c == h)))
            def _():
                slice_copy(index, h).wait_send()

    for kind in range(2):
        for g in range(EXPERTS):

            @pl.when(host_of(g)[0] != me)
            def _():
                row_copy(kind, g)[1].wait_send()

    for copy in residuals:
        copy.wait_send()
    for place in range(4):
        for index in range(3):
            sibling_copy(place, index).wait_send()
    for n in range(2):
        for index in range(3):
            host_copy(n, index).wait_send()
    for q in range(n_src):
        back_copy(q, *up_args).wait_send()
        back_copy(q, *dn_args).wait_send()


def per_device(
    act_up, routes_up, gates_up, saved_down, grad_down, routes_down, gates_down, norm_gain, w_gate, w_up, w_down,
):
    tokens, features = act_up.shape[1:]
    hidden = w_gate.shape[3]
    half = features // 2
    rows = EXPERTS * BLOCK
    vmem = pl.BlockSpec(memory_space=pltpu.VMEM)
    hbm = pl.BlockSpec(memory_space=pl.ANY)
    dma = pltpu.SemaphoreType.DMA
    up, down = pl.pallas_call(
        kernel,
        out_shape=(jax.ShapeDtypeStruct((tokens, features), BF16),) * 2,
        in_specs=[vmem] * 8 + [hbm] * 3,
        out_specs=(vmem, vmem),
        scratch_shapes=[
            pltpu.VMEM((SLICES, features, hidden), BF16),
            pltpu.VMEM((SLICES, features, hidden), BF16),
            pltpu.VMEM((SLICES, hidden, features), BF16),
            pltpu.VMEM((2 * tokens, half), BF16),
            pltpu.VMEM((2 * tokens, features), BF16),
            pltpu.VMEM((rows, half), BF16),
            pltpu.VMEM((rows, features), BF16),
            pltpu.VMEM((rows, half), BF16),
            pltpu.VMEM((rows, features), BF16),
            pltpu.VMEM((EXPERTS * CAP, features), BF16),
            pltpu.VMEM((EXPERTS * CAP, features), BF16),
            pltpu.VMEM((EXPERTS * CAP, features), BF16),
            pltpu.VMEM((EXPERTS * CAP, features), F32),
            pltpu.VMEM((EXPERTS * CAP, features), F32),
            pltpu.VMEM((rows, half), BF16),
            pltpu.VMEM((rows, half), BF16),
            pltpu.VMEM((rows, half), BF16),
            pltpu.VMEM((rows, half), BF16),
            pltpu.VMEM((tokens, features), BF16),
            pltpu.VMEM((tokens, features), BF16),
            pltpu.VMEM((tokens, features), BF16),
            pltpu.VMEM((1, features), F32),
            pltpu.VMEM((1, tokens), jnp.int32),
            pltpu.VMEM((1, tokens), F32),
            pltpu.VMEM((1, tokens), jnp.int32),
            pltpu.VMEM((1, tokens), F32),
            dma((2, EXPERTS)),
            dma((2, EXPERTS)),
            dma((3, 2)),
            dma((SLICES, 3, 2)),
            dma((SLICES, 3)),
            dma((2, 3)),
            dma((EXPERTS,)),
            dma((EXPERTS,)),
            dma((EXPERTS,)),
            dma((EXPERTS,)),
            dma((8,)),
            dma((8,)),
        ],
        compiler_params=pltpu.CompilerParams(
            collective_id=0, has_side_effects=True, vmem_limit_bytes=60 * MIB
        ),
        cost_estimate=pl.CostEstimate(flops=12_000_000_000, bytes_accessed=12_000_000, transcendentals=400_000),
    )(
        act_up[0], saved_down[0], grad_down[0], norm_gain,
        routes_up.reshape(1, tokens), gates_up.reshape(1, tokens),
        routes_down.reshape(1, tokens), gates_down.reshape(1, tokens),
        w_gate[0, 0], w_up[0, 0], w_down[0, 0],
    )
    return up[None], down[None]


def solution(mesh):
    tokens = P("section", "expert", None)
    weights = P("section", "expert", None, None)
    return jax.shard_map(
        per_device,
        mesh=mesh,
        in_specs=(tokens,) * 7 + (P("section", None),) + (weights,) * 3,
        out_specs=(tokens, tokens),
        check_vma=False,
    )
```

```python
import functools

import jax
import jax.numpy as jnp
from jax import lax
from jax.experimental import pallas as pl
from jax.experimental.pallas import tpu as pltpu
from jax.sharding import PartitionSpec as P

EPS = 1e-06
CAP = 24
BLOCK = 2 * CAP
EXPERTS = 8
SLICES = 4
MIB = 1024 * 1024
MESH = pl.DeviceIdType.MESH
F32 = jnp.float32
BF16 = jnp.bfloat16


def nearest(rel):
    inside = lax.rem(rel + 7, 8) // 4
    second = 1 - inside
    dist = second * (rel - 1) + inside * lax.rem(8 - rel, 8)
    return second, dist


def expert_home(zl, yh, c):
    return zl * 4 + yh * 2 + c


def column(row):
    n = row.shape[1]
    eye = lax.broadcasted_iota(jnp.int32, (n, n), 0) == lax.broadcasted_iota(jnp.int32, (n, n), 1)
    return jnp.sum(jnp.where(eye, row, 0.0), axis=1, keepdims=True)


def block_rows(route_row):
    n = route_row.shape[1]
    earlier = lax.broadcasted_iota(jnp.int32, (n, n), 0) < lax.broadcasted_iota(jnp.int32, (n, n), 1)
    same = jnp.logical_and(column(route_row) == route_row, earlier)
    slot = jnp.sum(jnp.where(same, 1.0, 0.0), axis=0, keepdims=True)
    return route_row * float(BLOCK) + slot


def contract_last(a, b):
    return lax.dot_general(a, b, (((1,), (1,)), ((), ())), preferred_element_type=F32)


def kernel(
    act, saved, grad, gain, route_up, weight_up, route_dn, weight_dn, wg_in, wu_in, wd_in,
    out_up, out_dn,
    wg, wu, wd, table_up, table_dn, packed_up, packed_dn, rows_up, rows_dn, x_up, x_dn, g_dn, acc_up, acc_dn,
    back_up_out, back_dn_out, back_up_in, back_dn_in,
    act_in, saved_in, grad_in, gain_in, route_up_in, weight_up_in, route_dn_in, weight_dn_in,
    row_send, row_recv, src_send, w_recv, sib_send, fwd_send,
    up_send, up_recv, dn_send, dn_recv, res_send, res_recv,
):
    tokens, features = act.shape
    half = features // 2
    hidden = wg_in.shape[1]
    n_sec = lax.axis_size("section")
    sec = lax.axis_index("section")
    me = lax.axis_index("expert")
    z, yh, c = me // 4, lax.rem(me // 2, 2), lax.rem(me, 2)
    after = lax.rem(sec + 1, n_sec)
    before = lax.rem(sec + n_sec - 1, n_sec)

    own_zl = lax.rem(z, 2)
    own_first = 2 * (2 * c + own_zl)
    own_rel = lax.rem(z - own_first + 8, 8)
    own_second, _ = nearest(own_rel)
    own_host = own_first + own_second
    m = own_rel // 2
    own_place = (1 - own_zl) * (m + m // 2 - 2 * (m // 3)) + own_zl * (2 * m - m // 2 - 4 * (m // 3))

    pair = z // 2
    side = lax.rem(z, 2)
    host_zl, host_c = lax.rem(pair, 2), pair // 2
    host_expert = expert_home(host_zl, yh, host_c)
    other_host = (2 * pair + 1 - side) * 4 + yh * 2 + c
    sibling = z * 4 + yh * 2 + 1 - c
    leads_even = 1 - lax.rem(host_zl + side, 2)

    def source(dist, src_yh):
        src_z = lax.rem(2 * pair + side + (2 * side - 1) * dist + 8, 8)
        return src_z * 4 + src_yh * 2 + c

    def host_of(g):
        zl, g_yh, g_c = g // 4, (g // 2) % 2, g % 2
        first = 2 * (2 * g_c + zl)
        second, dist = nearest(lax.rem(z - first + 8, 8))
        return (first + second) * 4 + g_yh * 2 + c, dist * 2 + yh

    def slice_source(place):
        rel = (1 - host_zl) * (0, 2, 6, 4)[place] + host_zl * (1, 7, 3, 5)[place]
        return lax.rem(2 * pair + rel, 8) * 4 + yh * 2 + host_c

    barrier = pltpu.get_barrier_semaphore()

    def greet(section, peer):
        pl.semaphore_signal(barrier, inc=1, device_id=(section, peer), device_id_type=MESH)

    for dist in range(4):
        for src_yh in range(2):
            peer = source(dist, src_yh)

            @pl.when(peer != me)
            def _():
                greet(sec, peer)

    for place in range(4):
        peer = slice_source(place)
        leads = leads_even if place % 2 == 0 else 1 - leads_even

        @pl.when(jnp.logical_and(leads == 1, peer != me))
        def _():
            greet(sec, peer)

    greet(sec, other_host)
    greet(sec, sibling)
    greet(before, me)
    greet(after, me)
    mats = ((wg_in, wg), (wu_in, wu), (wd_in, wd))

    def w_half(ref, index, h):
        size = mats[index][0].shape[0] // 2
        return ref.at[pl.ds(pl.multiple_of(h * size, 128), size)]

    def remote(src, dst, send, recv, section, peer):
        return pltpu.make_async_remote_copy(
            src_ref=src, dst_ref=dst, send_sem=send, recv_sem=recv,
            device_id=(section, peer), device_id_type=MESH,
        )

    gain_row = gain[...]
    rows_step = 16

    def normed(ref, at):
        values = ref[at, :].astype(F32)
        scaling = lax.rsqrt(jnp.mean(values * values, axis=-1, keepdims=True) + EPS)
        return (values * scaling * gain_row).astype(BF16)

    def norm_up(step, _):
        at = pl.ds(pl.multiple_of(step * rows_step, rows_step), rows_step)
        to = pl.ds(pl.multiple_of(tokens + step * rows_step, rows_step), rows_step)
        rows = normed(act, at)
        table_up[at, :] = rows[:, :half]
        table_up[to, :] = rows[:, half:]
        return 0

    def norm_dn(step, _):
        at = pl.ds(pl.multiple_of(step * rows_step, rows_step), rows_step)
        table_dn[at, :] = normed(saved, at)
        return 0

    n_rows = EXPERTS * BLOCK
    width = 256

    def pack(route_row, table, packed):
        at = block_rows(route_row)
        row_index = lax.broadcasted_iota(jnp.int32, (n_rows, 2 * tokens), 0).astype(F32)
        pick = (row_index == jnp.concatenate([at, at + float(CAP)], axis=1)).astype(BF16)

        def body(step, _):
            at = pl.ds(pl.multiple_of(step * width, width), width)
            packed[:, at] = jnp.dot(pick, table[:, at], preferred_element_type=F32).astype(BF16)
            return 0

        lax.fori_loop(0, packed.shape[1] // width, body, 0)

    def row_block(ref, index):
        return ref.at[pl.ds(pl.multiple_of(index * BLOCK, BLOCK), BLOCK)]

    kinds = ((packed_up, rows_up), (packed_dn, rows_dn))

    def row_copy(kind, g):
        packed, rows = kinds[kind]
        peer, slot = host_of(g)
        return peer, remote(
            row_block(packed, g), row_block(rows, slot), row_send.at[kind, g], row_recv.at[kind, slot], sec, peer
        )

    def send_rows(kind, dists=(3, 2, 1, 0)):
        packed, rows = kinds[kind]
        half_z, odd = z // 2, lax.rem(z, 2)
        for dist in dists:
            step = (0, 3, 1, 2)[dist] * (1 - odd) + (0, 1, 3, 2)[dist] * odd
            to = lax.rem(half_z + step, 4)
            for g_yh in range(2):
                g = lax.rem(to, 2) * 4 + g_yh * 2 + to // 2
                peer = (2 * to + nearest(lax.rem(z - 2 * to + 8, 8))[0]) * 4 + g_yh * 2 + c
                slot = dist * 2 + yh
                copy = remote(
                    row_block(packed, g), row_block(rows, slot),
                    row_send.at[kind, g], row_recv.at[kind, slot], sec, peer,
                )
                if dist:
                    copy.start()
                    continue

                @pl.when(peer == me)
                def _():
                    pltpu.make_async_copy(
                        row_block(packed, g), row_block(rows, slot), row_recv.at[kind, slot]
                    ).start()

                @pl.when(peer != me)
                def _():
                    copy.start()

    def wait_rows(kind):
        rows = kinds[kind][1]
        for slot in range(EXPERTS):
            view = row_block(rows, slot)
            remote(view, view, row_send.at[kind, slot], row_recv.at[kind, slot], sec, sibling).wait_recv()

    lax.fori_loop(0, tokens // rows_step, norm_up, 0)
    pack(route_up[...].astype(F32), table_up, packed_up)
    here = jnp.where(own_host == z, 1, 0)
    pl.semaphore_wait(barrier, 13 - here)

    def slice_copy(index, h):
        src, dst = mats[index]
        return remote(
            w_half(src, index, h), w_half(dst.at[own_place], index, h),
            src_send.at[index, h], w_recv.at[own_place, index, h], sec, own_host * 4 + yh * 2 + h,
        )

    for index in range(3):
        for h in range(2):
            mine = jnp.logical_and(own_host == z, c == h)

            @pl.when(mine)
            def _():
                src, dst = mats[index]
                pltpu.make_async_copy(
                    w_half(src, index, h), w_half(dst.at[own_place], index, h), w_recv.at[own_place, index, h]
                ).start()

            @pl.when(jnp.logical_not(mine))
            def _():
                slice_copy(index, h).start()

    send_rows(0)
    lax.fori_loop(0, tokens // rows_step, norm_dn, 0)
    table_dn[tokens:, :] = grad[...]
    pack(route_dn[...].astype(F32), table_dn, packed_dn)

    residuals = [
        remote(act, act_in, res_send.at[0], res_recv.at[0], after, me),
        remote(route_up, route_up_in, res_send.at[1], res_recv.at[1], after, me),
        remote(weight_up, weight_up_in, res_send.at[6], res_recv.at[6], after, me),
        remote(saved, saved_in, res_send.at[2], res_recv.at[2], before, me),
        remote(grad, grad_in, res_send.at[3], res_recv.at[3], before, me),
        remote(gain, gain_in, res_send.at[4], res_recv.at[4], before, me),
        remote(route_dn, route_dn_in, res_send.at[5], res_recv.at[5], before, me),
        remote(weight_dn, weight_dn_in, res_send.at[7], res_recv.at[7], before, me),
    ]

    acc_up[...] = jnp.zeros_like(acc_up)
    acc_dn[...] = jnp.zeros_like(acc_dn)

    def half_copy(place, index, h, send, peer):
        view = w_half(mats[index][1].at[place], index, h)
        return remote(view, view, send, w_recv.at[place, index, h], sec, peer)

    def sibling_copy(place, index):
        return half_copy(place, index, c, sib_send.at[place, index], sibling)

    def host_copy(n, index):
        return half_copy(lead_place(n), index, c, fwd_send.at[n, index], other_host)

    def lead_place(n):
        return 2 * n + 1 - leads_even

    def follow_place(n):
        return 2 * n + leads_even

    def lead(n):
        for index in range(3):
            sibling_copy(lead_place(n), index).wait_recv()
            host_copy(n, index).start()
            sibling_copy(lead_place(n), index).start()

    def follow(n):
        for index in range(3):
            sibling_copy(follow_place(n), index).wait_recv()
            sibling_copy(follow_place(n), index).start()

    def wait_sibling(place):
        for index in range(3):
            half_copy(place, index, 1 - c, sib_send.at[place, index], sibling).wait_recv()

    n_src = EXPERTS

    def arrange(rows, low, high):
        def body(step, _):
            top = rows[pl.ds(pl.multiple_of(step * 2 * BLOCK, 2 * BLOCK), BLOCK), :].astype(F32)
            bottom = rows[pl.ds(pl.multiple_of((step * 2 + 1) * BLOCK, BLOCK), BLOCK), :].astype(F32)
            at = pl.ds(pl.multiple_of(step * BLOCK, BLOCK), BLOCK)
            low[at, :rows.shape[1]] = jnp.concatenate([top[:CAP], bottom[:CAP]], axis=0).astype(BF16)
            second = jnp.concatenate([top[CAP:], bottom[CAP:]], axis=0).astype(BF16)
            if high is None:
                low[at, rows.shape[1]:] = second
            else:
                high[at, :] = second
            return 0

        lax.fori_loop(0, n_src // 2, body, 0)

    def send_back(dists, acc, out, send, recv, section, into):
        for dist in dists:
            for src_yh in range(2):
                q = dist * 2 + src_yh
                both = jnp.concatenate(
                    [acc[q * CAP:(q + 1) * CAP, :half], acc[q * CAP:(q + 1) * CAP, half:]], axis=0
                )
                out[q * BLOCK:(q + 1) * BLOCK, :] = both.astype(BF16)
                back_copy(q, out, send, recv, section, into).start()

    def back_copy(q, out, send, recv, section, into):
        return remote(
            row_block(out, q), row_block(into, host_expert), send.at[q], recv.at[host_expert],
            section, source(q // 2, q % 2),
        )

    up_args = (back_up_out, up_send, up_recv, after, back_up_in)
    dn_args = (back_dn_out, dn_send, dn_recv, before, back_dn_in)

    def use_up(place, rows):
        x = x_up[rows, :]
        gate = jnp.dot(x, wg[place], preferred_element_type=F32)
        upper = jnp.dot(x, wu[place], preferred_element_type=F32)
        middle = (jax.nn.silu(gate) * upper).astype(BF16)

        def add_up(step, _):
            at = pl.ds(pl.multiple_of(step * width, width), width)
            acc_up[rows, at] += jnp.dot(middle, wd[place, :, at], preferred_element_type=F32)
            return 0

        lax.fori_loop(0, features // width, add_up, 0)

    def use_dn(place, rows):
        x = x_dn[rows, :]
        gate = jnp.dot(x, wg[place], preferred_element_type=F32)
        upper = jnp.dot(x, wu[place], preferred_element_type=F32)
        pulled = contract_last(g_dn[rows, :], wd[place])
        sigma = jax.nn.sigmoid(gate)
        d_gate = (pulled * upper * sigma * (1.0 + gate * (1.0 - sigma))).astype(BF16)
        d_upper = (pulled * gate * sigma).astype(BF16)

        def add_dn(step, _):
            at = pl.ds(pl.multiple_of(step * width, width), width)
            acc_dn[rows, at] += contract_last(d_gate, wg[place, at, :]) + contract_last(d_upper, wu[place, at, :])
            return 0

        lax.fori_loop(0, features // width, add_dn, 0)

    def at_step(step):
        return 2 * (step // 2) + 1 - leads_even + lax.rem(step, 2) * (2 * leads_even - 1)

    def loop(use, first, end, rows):
        def body(step, _):
            use(at_step(step), rows)
            return 0

        lax.fori_loop(first, end, body, 0)

    lead(0)
    send_rows(1, (1, 0))
    lead(1)
    send_rows(1, (3,))
    follow(0)
    for copy in residuals:
        copy.start()

    wait_rows(0)
    arrange(rows_up, x_up, None)
    send_rows(1, (2,))
    for place in (lead_place(0), lead_place(1), follow_place(0)):
        wait_sibling(place)
    part = n_src * CAP // 2
    near, far = pl.ds(0, part), pl.ds(part, part)
    loop(use_up, 0, 3, pl.ds(0, 2 * part))
    follow(1)
    wait_sibling(follow_place(1))
    loop(use_up, 3, 4, far)
    send_back((3, 2), acc_up, *up_args)
    loop(use_up, 3, 4, near)
    send_back((1, 0), acc_up, *up_args)
    wait_rows(1)
    arrange(rows_dn, x_dn, g_dn)
    loop(use_dn, 0, 4, far)
    send_back((3, 2), acc_dn, *dn_args)
    loop(use_dn, 0, 4, near)
    send_back((1, 0), acc_dn, *dn_args)

    for copy in residuals:
        copy.wait_recv()

    def unpick(route_row):
        lane = lax.broadcasted_iota(jnp.int32, (tokens, n_rows), 1).astype(F32)
        at = column(block_rows(route_row))
        return jnp.concatenate([lane == at, lane == at + float(CAP)], axis=0).astype(BF16)

    def wait_back(out, send, recv, section, into):
        for g in range(EXPERTS):
            remote(
                row_block(into, g), row_block(into, g), send.at[g], recv.at[g], section, me
            ).wait_recv()

    wait_back(*up_args)
    pick_up = unpick(route_up_in[...].astype(F32))
    gate_up_col = column(weight_up_in[...])

    def finish_up(step, _):
        at = pl.ds(pl.multiple_of(step * width, width), width)
        back = jnp.dot(pick_up, back_up_in[:, at], preferred_element_type=F32)
        for h in range(2):
            to = pl.ds(pl.multiple_of(h * half + step * width, width), width)
            mixed = back[h * tokens:(h + 1) * tokens] * gate_up_col
            out_up[:, to] = (act_in[:, to].astype(F32) + mixed).astype(BF16)
        return 0

    lax.fori_loop(0, half // width, finish_up, 0)

    wait_back(*dn_args)
    pick_dn = unpick(route_dn_in[...].astype(F32))
    gate_dn_col = column(weight_dn_in[...])

    def pull_dn(step, carry):
        squares, dots = carry
        at = pl.ds(pl.multiple_of(step * width, width), width)
        back = jnp.dot(pick_dn, back_dn_in[:, at], preferred_element_type=F32)
        for h in range(2):
            to = pl.ds(pl.multiple_of(h * half + step * width, width), width)
            u = back[h * tokens:(h + 1) * tokens] * gate_dn_col * gain_in[0:1, to]
            acc_dn[:tokens, to] = u
            x = saved_in[:, to].astype(F32)
            squares = squares + jnp.sum(x * x, axis=-1, keepdims=True)
            dots = dots + jnp.sum(x * u, axis=-1, keepdims=True)
        return squares, dots

    zero = jnp.zeros((tokens, 1), F32)
    squares, dots = lax.fori_loop(0, half // width, pull_dn, (zero, zero))
    r = lax.rsqrt(squares / features + EPS)
    pull = r * r * r * (dots / features)

    def finish_dn(step, _):
        to = pl.ds(pl.multiple_of(step * width, width), width)
        x = saved_in[:, to].astype(F32)
        out_dn[:, to] = (grad_in[:, to].astype(F32) + r * acc_dn[:tokens, to] - x * pull).astype(BF16)
        return 0

    lax.fori_loop(0, features // width, finish_dn, 0)

    for index in range(3):
        for h in range(2):

            @pl.when(jnp.logical_not(jnp.logical_and(own_host == z, c == h)))
            def _():
                slice_copy(index, h).wait_send()

    for kind in range(2):
        for g in range(EXPERTS):

            @pl.when(host_of(g)[0] != me)
            def _():
                row_copy(kind, g)[1].wait_send()

    for copy in residuals:
        copy.wait_send()
    for place in range(4):
        for index in range(3):
            sibling_copy(place, index).wait_send()
    for n in range(2):
        for index in range(3):
            host_copy(n, index).wait_send()
    for q in range(n_src):
        back_copy(q, *up_args).wait_send()
        back_copy(q, *dn_args).wait_send()


def per_device(
    act_up, routes_up, gates_up, saved_down, grad_down, routes_down, gates_down, norm_gain, w_gate, w_up, w_down,
):
    tokens, features = act_up.shape[1:]
    hidden = w_gate.shape[3]
    half = features // 2
    rows = EXPERTS * BLOCK
    vmem = pl.BlockSpec(memory_space=pltpu.VMEM)
    hbm = pl.BlockSpec(memory_space=pl.ANY)
    dma = pltpu.SemaphoreType.DMA
    up, down = pl.pallas_call(
        kernel,
        out_shape=(jax.ShapeDtypeStruct((tokens, features), BF16),) * 2,
        in_specs=[vmem] * 8 + [hbm] * 3,
        out_specs=(vmem, vmem),
        scratch_shapes=[
            pltpu.VMEM((SLICES, features, hidden), BF16),
            pltpu.VMEM((SLICES, features, hidden), BF16),
            pltpu.VMEM((SLICES, hidden, features), BF16),
            pltpu.VMEM((2 * tokens, half), BF16),
            pltpu.VMEM((2 * tokens, features), BF16),
            pltpu.VMEM((rows, half), BF16),
            pltpu.VMEM((rows, features), BF16),
            pltpu.VMEM((rows, half), BF16),
            pltpu.VMEM((rows, features), BF16),
            pltpu.VMEM((EXPERTS * CAP, features), BF16),
            pltpu.VMEM((EXPERTS * CAP, features), BF16),
            pltpu.VMEM((EXPERTS * CAP, features), BF16),
            pltpu.VMEM((EXPERTS * CAP, features), F32),
            pltpu.VMEM((EXPERTS * CAP, features), F32),
            pltpu.VMEM((rows, half), BF16),
            pltpu.VMEM((rows, half), BF16),
            pltpu.VMEM((rows, half), BF16),
            pltpu.VMEM((rows, half), BF16),
            pltpu.VMEM((tokens, features), BF16),
            pltpu.VMEM((tokens, features), BF16),
            pltpu.VMEM((tokens, features), BF16),
            pltpu.VMEM((1, features), F32),
            pltpu.VMEM((1, tokens), jnp.int32),
            pltpu.VMEM((1, tokens), F32),
            pltpu.VMEM((1, tokens), jnp.int32),
            pltpu.VMEM((1, tokens), F32),
            dma((2, EXPERTS)),
            dma((2, EXPERTS)),
            dma((3, 2)),
            dma((SLICES, 3, 2)),
            dma((SLICES, 3)),
            dma((2, 3)),
            dma((EXPERTS,)),
            dma((EXPERTS,)),
            dma((EXPERTS,)),
            dma((EXPERTS,)),
            dma((8,)),
            dma((8,)),
        ],
        compiler_params=pltpu.CompilerParams(
            collective_id=0, has_side_effects=True, vmem_limit_bytes=60 * MIB
        ),
        cost_estimate=pl.CostEstimate(flops=12_000_000_000, bytes_accessed=12_000_000, transcendentals=400_000),
    )(
        act_up[0], saved_down[0], grad_down[0], norm_gain,
        routes_up.reshape(1, tokens), gates_up.reshape(1, tokens),
        routes_down.reshape(1, tokens), gates_down.reshape(1, tokens),
        w_gate[0, 0], w_up[0, 0], w_down[0, 0],
    )
    return up[None], down[None]


def solution(mesh):
    tokens = P("section", "expert", None)
    weights = P("section", "expert", None, None)
    return jax.shard_map(
        per_device,
        mesh=mesh,
        in_specs=(tokens,) * 7 + (P("section", None),) + (weights,) * 3,
        out_specs=(tokens, tokens),
        check_vma=False,
    )
```

```python
import functools

import jax
import jax.numpy as jnp
from jax import lax
from jax.experimental import pallas as pl
from jax.experimental.pallas import tpu as pltpu
from jax.sharding import PartitionSpec as P

EPS = 1e-06
CAP = 24
BLOCK = 2 * CAP
EXPERTS = 8
SLICES = 4
MIB = 1024 * 1024
MESH = pl.DeviceIdType.MESH
F32 = jnp.float32
BF16 = jnp.bfloat16


def nearest(rel):
    inside = lax.rem(rel + 7, 8) // 4
    second = 1 - inside
    dist = second * (rel - 1) + inside * lax.rem(8 - rel, 8)
    return second, dist


def expert_home(zl, yh, c):
    return zl * 4 + yh * 2 + c


def column(row):
    n = row.shape[1]
    eye = lax.broadcasted_iota(jnp.int32, (n, n), 0) == lax.broadcasted_iota(jnp.int32, (n, n), 1)
    return jnp.sum(jnp.where(eye, row, 0.0), axis=1, keepdims=True)


def block_rows(route_row):
    n = route_row.shape[1]
    earlier = lax.broadcasted_iota(jnp.int32, (n, n), 0) < lax.broadcasted_iota(jnp.int32, (n, n), 1)
    same = jnp.logical_and(column(route_row) == route_row, earlier)
    slot = jnp.sum(jnp.where(same, 1.0, 0.0), axis=0, keepdims=True)
    return route_row * float(BLOCK) + slot


def contract_last(a, b):
    return lax.dot_general(a, b, (((1,), (1,)), ((), ())), preferred_element_type=F32)


def kernel(
    act, saved, grad, gain, route_up, weight_up, route_dn, weight_dn, wg_in, wu_in, wd_in,
    out_up, out_dn,
    wg, wu, wd, table_up, table_dn, packed_up, packed_dn, rows_up, rows_dn, x_up, x_dn, g_dn, acc_up, acc_dn,
    back_up_out, back_dn_out, back_up_in, back_dn_in,
    act_in, saved_in, grad_in, gain_in, route_up_in, weight_up_in, route_dn_in, weight_dn_in,
    row_send, row_recv, src_send, w_recv, sib_send, fwd_send,
    up_send, up_recv, dn_send, dn_recv, res_send, res_recv,
):
    tokens, features = act.shape
    half = features // 2
    hidden = wg_in.shape[1]
    n_sec = lax.axis_size("section")
    sec = lax.axis_index("section")
    me = lax.axis_index("expert")
    z, yh, c = me // 4, lax.rem(me // 2, 2), lax.rem(me, 2)
    after = lax.rem(sec + 1, n_sec)
    before = lax.rem(sec + n_sec - 1, n_sec)

    own_zl = lax.rem(z, 2)
    own_first = 2 * (2 * c + own_zl)
    own_rel = lax.rem(z - own_first + 8, 8)
    own_second, _ = nearest(own_rel)
    own_host = own_first + own_second
    m = own_rel // 2
    own_place = (1 - own_zl) * (m + m // 2 - 2 * (m // 3)) + own_zl * (2 * m - m // 2 - 4 * (m // 3))

    pair = z // 2
    side = lax.rem(z, 2)
    host_zl, host_c = lax.rem(pair, 2), pair // 2
    host_expert = expert_home(host_zl, yh, host_c)
    other_host = (2 * pair + 1 - side) * 4 + yh * 2 + c
    sibling = z * 4 + yh * 2 + 1 - c
    leads_even = 1 - lax.rem(host_zl + side, 2)

    def source(dist, src_yh):
        src_z = lax.rem(2 * pair + side + (2 * side - 1) * dist + 8, 8)
        return src_z * 4 + src_yh * 2 + c

    def host_of(g):
        zl, g_yh, g_c = g // 4, (g // 2) % 2, g % 2
        first = 2 * (2 * g_c + zl)
        second, dist = nearest(lax.rem(z - first + 8, 8))
        return (first + second) * 4 + g_yh * 2 + c, dist * 2 + yh

    def slice_source(place):
        rel = (1 - host_zl) * (0, 2, 6, 4)[place] + host_zl * (1, 7, 3, 5)[place]
        return lax.rem(2 * pair + rel, 8) * 4 + yh * 2 + host_c

    barrier = pltpu.get_barrier_semaphore()

    def greet(section, peer):
        pl.semaphore_signal(barrier, inc=1, device_id=(section, peer), device_id_type=MESH)

    for dist in range(4):
        for src_yh in range(2):
            peer = source(dist, src_yh)

            @pl.when(peer != me)
            def _():
                greet(sec, peer)

    for place in range(4):
        peer = slice_source(place)
        leads = leads_even if place % 2 == 0 else 1 - leads_even

        @pl.when(jnp.logical_and(leads == 1, peer != me))
        def _():
            greet(sec, peer)

    greet(sec, other_host)
    greet(sec, sibling)
    greet(before, me)
    greet(after, me)
    mats = ((wg_in, wg), (wu_in, wu), (wd_in, wd))

    def w_half(ref, index, h):
        size = mats[index][0].shape[0] // 2
        return ref.at[pl.ds(pl.multiple_of(h * size, 128), size)]

    def remote(src, dst, send, recv, section, peer):
        return pltpu.make_async_remote_copy(
            src_ref=src, dst_ref=dst, send_sem=send, recv_sem=recv,
            device_id=(section, peer), device_id_type=MESH,
        )

    gain_row = gain[...]
    rows_step = 16

    def normed(ref, at):
        values = ref[at, :].astype(F32)
        scaling = lax.rsqrt(jnp.mean(values * values, axis=-1, keepdims=True) + EPS)
        return (values * scaling * gain_row).astype(BF16)

    def norm_up(step, _):
        at = pl.ds(pl.multiple_of(step * rows_step, rows_step), rows_step)
        to = pl.ds(pl.multiple_of(tokens + step * rows_step, rows_step), rows_step)
        rows = normed(act, at)
        table_up[at, :] = rows[:, :half]
        table_up[to, :] = rows[:, half:]
        return 0

    def norm_dn(step, _):
        at = pl.ds(pl.multiple_of(step * rows_step, rows_step), rows_step)
        table_dn[at, :] = normed(saved, at)
        return 0

    n_rows = EXPERTS * BLOCK
    width = 256

    def pack(route_row, table, packed):
        at = block_rows(route_row)
        row_index = lax.broadcasted_iota(jnp.int32, (n_rows, 2 * tokens), 0).astype(F32)
        pick = (row_index == jnp.concatenate([at, at + float(CAP)], axis=1)).astype(BF16)

        def body(step, _):
            at = pl.ds(pl.multiple_of(step * width, width), width)
            packed[:, at] = jnp.dot(pick, table[:, at], preferred_element_type=F32).astype(BF16)
            return 0

        lax.fori_loop(0, packed.shape[1] // width, body, 0)

    def row_block(ref, index):
        return ref.at[pl.ds(pl.multiple_of(index * BLOCK, BLOCK), BLOCK)]

    kinds = ((packed_up, rows_up), (packed_dn, rows_dn))

    def row_copy(kind, g):
        packed, rows = kinds[kind]
        peer, slot = host_of(g)
        return peer, remote(
            row_block(packed, g), row_block(rows, slot), row_send.at[kind, g], row_recv.at[kind, slot], sec, peer
        )

    def send_rows(kind, dists=(3, 2, 1, 0)):
        packed, rows = kinds[kind]
        half_z, odd = z // 2, lax.rem(z, 2)
        for dist in dists:
            step = (0, 3, 1, 2)[dist] * (1 - odd) + (0, 1, 3, 2)[dist] * odd
            to = lax.rem(half_z + step, 4)
            for g_yh in range(2):
                g = lax.rem(to, 2) * 4 + g_yh * 2 + to // 2
                peer = (2 * to + nearest(lax.rem(z - 2 * to + 8, 8))[0]) * 4 + g_yh * 2 + c
                slot = dist * 2 + yh
                copy = remote(
                    row_block(packed, g), row_block(rows, slot),
                    row_send.at[kind, g], row_recv.at[kind, slot], sec, peer,
                )
                if dist:
                    copy.start()
                    continue

                @pl.when(peer == me)
                def _():
                    pltpu.make_async_copy(
                        row_block(packed, g), row_block(rows, slot), row_recv.at[kind, slot]
                    ).start()

                @pl.when(peer != me)
                def _():
                    copy.start()

    def wait_rows(kind):
        rows = kinds[kind][1]
        for slot in range(EXPERTS):
            view = row_block(rows, slot)
            remote(view, view, row_send.at[kind, slot], row_recv.at[kind, slot], sec, sibling).wait_recv()

    lax.fori_loop(0, tokens // rows_step, norm_up, 0)
    pack(route_up[...].astype(F32), table_up, packed_up)
    here = jnp.where(own_host == z, 1, 0)
    pl.semaphore_wait(barrier, 13 - here)

    def slice_copy(index, h):
        src, dst = mats[index]
        return remote(
            w_half(src, index, h), w_half(dst.at[own_place], index, h),
            src_send.at[index, h], w_recv.at[own_place, index, h], sec, own_host * 4 + yh * 2 + h,
        )

    for index in range(3):
        for h in range(2):
            mine = jnp.logical_and(own_host == z, c == h)

            @pl.when(mine)
            def _():
                src, dst = mats[index]
                pltpu.make_async_copy(
                    w_half(src, index, h), w_half(dst.at[own_place], index, h), w_recv.at[own_place, index, h]
                ).start()

            @pl.when(jnp.logical_not(mine))
            def _():
                slice_copy(index, h).start()

    send_rows(0)
    lax.fori_loop(0, tokens // rows_step, norm_dn, 0)
    table_dn[tokens:, :] = grad[...]
    pack(route_dn[...].astype(F32), table_dn, packed_dn)

    residuals = [
        remote(act, act_in, res_send.at[0], res_recv.at[0], after, me),
        remote(route_up, route_up_in, res_send.at[1], res_recv.at[1], after, me),
        remote(weight_up, weight_up_in, res_send.at[6], res_recv.at[6], after, me),
        remote(saved, saved_in, res_send.at[2], res_recv.at[2], before, me),
        remote(grad, grad_in, res_send.at[3], res_recv.at[3], before, me),
        remote(gain, gain_in, res_send.at[4], res_recv.at[4], before, me),
        remote(route_dn, route_dn_in, res_send.at[5], res_recv.at[5], before, me),
        remote(weight_dn, weight_dn_in, res_send.at[7], res_recv.at[7], before, me),
    ]

    acc_up[...] = jnp.zeros_like(acc_up)
    acc_dn[...] = jnp.zeros_like(acc_dn)

    def half_copy(place, index, h, send, peer):
        view = w_half(mats[index][1].at[place], index, h)
        return remote(view, view, send, w_recv.at[place, index, h], sec, peer)

    def sibling_copy(place, index):
        return half_copy(place, index, c, sib_send.at[place, index], sibling)

    def host_copy(n, index):
        return half_copy(lead_place(n), index, c, fwd_send.at[n, index], other_host)

    def lead_place(n):
        return 2 * n + 1 - leads_even

    def follow_place(n):
        return 2 * n + leads_even

    def lead(n):
        for index in range(3):
            sibling_copy(lead_place(n), index).wait_recv()
            host_copy(n, index).start()
            sibling_copy(lead_place(n), index).start()

    def follow(n):
        for index in range(3):
            sibling_copy(follow_place(n), index).wait_recv()
            sibling_copy(follow_place(n), index).start()

    def wait_sibling(place):
        for index in range(3):
            half_copy(place, index, 1 - c, sib_send.at[place, index], sibling).wait_recv()

    n_src = EXPERTS

    def arrange(rows, low, high):
        def body(step, _):
            top = rows[pl.ds(pl.multiple_of(step * 2 * BLOCK, 2 * BLOCK), BLOCK), :].astype(F32)
            bottom = rows[pl.ds(pl.multiple_of((step * 2 + 1) * BLOCK, BLOCK), BLOCK), :].astype(F32)
            at = pl.ds(pl.multiple_of(step * BLOCK, BLOCK), BLOCK)
            low[at, :rows.shape[1]] = jnp.concatenate([top[:CAP], bottom[:CAP]], axis=0).astype(BF16)
            second = jnp.concatenate([top[CAP:], bottom[CAP:]], axis=0).astype(BF16)
            if high is None:
                low[at, rows.shape[1]:] = second
            else:
                high[at, :] = second
            return 0

        lax.fori_loop(0, n_src // 2, body, 0)

    def send_back(dists, acc, out, send, recv, section, into):
        for dist in dists:
            for src_yh in range(2):
                q = dist * 2 + src_yh
                both = jnp.concatenate(
                    [acc[q * CAP:(q + 1) * CAP, :half], acc[q * CAP:(q + 1) * CAP, half:]], axis=0
                )
                out[q * BLOCK:(q + 1) * BLOCK, :] = both.astype(BF16)
                back_copy(q, out, send, recv, section, into).start()

    def back_copy(q, out, send, recv, section, into):
        return remote(
            row_block(out, q), row_block(into, host_expert), send.at[q], recv.at[host_expert],
            section, source(q // 2, q % 2),
        )

    up_args = (back_up_out, up_send, up_recv, after, back_up_in)
    dn_args = (back_dn_out, dn_send, dn_recv, before, back_dn_in)

    def use_up(place, rows):
        x = x_up[rows, :]
        gate = jnp.dot(x, wg[place], preferred_element_type=F32)
        upper = jnp.dot(x, wu[place], preferred_element_type=F32)
        middle = (jax.nn.silu(gate) * upper).astype(BF16)

        def add_up(step, _):
            at = pl.ds(pl.multiple_of(step * width, width), width)
            acc_up[rows, at] += jnp.dot(middle, wd[place, :, at], preferred_element_type=F32)
            return 0

        lax.fori_loop(0, features // width, add_up, 0)

    def use_dn(place, rows):
        x = x_dn[rows, :]
        gate = jnp.dot(x, wg[place], preferred_element_type=F32)
        upper = jnp.dot(x, wu[place], preferred_element_type=F32)
        pulled = contract_last(g_dn[rows, :], wd[place])
        sigma = jax.nn.sigmoid(gate)
        d_gate = (pulled * upper * sigma * (1.0 + gate * (1.0 - sigma))).astype(BF16)
        d_upper = (pulled * gate * sigma).astype(BF16)

        def add_dn(step, _):
            at = pl.ds(pl.multiple_of(step * width, width), width)
            acc_dn[rows, at] += contract_last(d_gate, wg[place, at, :]) + contract_last(d_upper, wu[place, at, :])
            return 0

        lax.fori_loop(0, features // width, add_dn, 0)

    def at_step(step):
        return 2 * (step // 2) + 1 - leads_even + lax.rem(step, 2) * (2 * leads_even - 1)

    def loop(use, first, end, rows):
        def body(step, _):
            use(at_step(step), rows)
            return 0

        lax.fori_loop(first, end, body, 0)

    lead(0)
    send_rows(1, (1, 0))
    lead(1)
    follow(0)
    send_rows(1, (3,))
    for copy in residuals:
        copy.start()

    wait_rows(0)
    arrange(rows_up, x_up, None)
    send_rows(1, (2,))
    for place in (lead_place(0), lead_place(1), follow_place(0)):
        wait_sibling(place)
    part = n_src * CAP // 2
    near, far = pl.ds(0, part), pl.ds(part, part)
    loop(use_up, 0, 3, pl.ds(0, 2 * part))
    follow(1)
    wait_sibling(follow_place(1))
    loop(use_up, 3, 4, far)
    send_back((3, 2), acc_up, *up_args)
    loop(use_up, 3, 4, near)
    send_back((1, 0), acc_up, *up_args)
    wait_rows(1)
    arrange(rows_dn, x_dn, g_dn)
    loop(use_dn, 0, 4, far)
    send_back((3, 2), acc_dn, *dn_args)
    loop(use_dn, 0, 4, near)
    send_back((1, 0), acc_dn, *dn_args)

    for copy in residuals:
        copy.wait_recv()

    def unpick(route_row):
        lane = lax.broadcasted_iota(jnp.int32, (tokens, n_rows), 1).astype(F32)
        at = column(block_rows(route_row))
        return jnp.concatenate([lane == at, lane == at + float(CAP)], axis=0).astype(BF16)

    def wait_back(out, send, recv, section, into):
        for g in range(EXPERTS):
            remote(
                row_block(into, g), row_block(into, g), send.at[g], recv.at[g], section, me
            ).wait_recv()

    wait_back(*up_args)
    pick_up = unpick(route_up_in[...].astype(F32))
    gate_up_col = column(weight_up_in[...])

    def finish_up(step, _):
        at = pl.ds(pl.multiple_of(step * width, width), width)
        back = jnp.dot(pick_up, back_up_in[:, at], preferred_element_type=F32)
        for h in range(2):
            to = pl.ds(pl.multiple_of(h * half + step * width, width), width)
            mixed = back[h * tokens:(h + 1) * tokens] * gate_up_col
            out_up[:, to] = (act_in[:, to].astype(F32) + mixed).astype(BF16)
        return 0

    lax.fori_loop(0, half // width, finish_up, 0)

    wait_back(*dn_args)
    pick_dn = unpick(route_dn_in[...].astype(F32))
    gate_dn_col = column(weight_dn_in[...])

    def pull_dn(step, carry):
        squares, dots = carry
        at = pl.ds(pl.multiple_of(step * width, width), width)
        back = jnp.dot(pick_dn, back_dn_in[:, at], preferred_element_type=F32)
        for h in range(2):
            to = pl.ds(pl.multiple_of(h * half + step * width, width), width)
            u = back[h * tokens:(h + 1) * tokens] * gate_dn_col * gain_in[0:1, to]
            acc_dn[:tokens, to] = u
            x = saved_in[:, to].astype(F32)
            squares = squares + jnp.sum(x * x, axis=-1, keepdims=True)
            dots = dots + jnp.sum(x * u, axis=-1, keepdims=True)
        return squares, dots

    zero = jnp.zeros((tokens, 1), F32)
    squares, dots = lax.fori_loop(0, half // width, pull_dn, (zero, zero))
    r = lax.rsqrt(squares / features + EPS)
    pull = r * r * r * (dots / features)

    def finish_dn(step, _):
        to = pl.ds(pl.multiple_of(step * width, width), width)
        x = saved_in[:, to].astype(F32)
        out_dn[:, to] = (grad_in[:, to].astype(F32) + r * acc_dn[:tokens, to] - x * pull).astype(BF16)
        return 0

    lax.fori_loop(0, features // width, finish_dn, 0)

    for index in range(3):
        for h in range(2):

            @pl.when(jnp.logical_not(jnp.logical_and(own_host == z, c == h)))
            def _():
                slice_copy(index, h).wait_send()

    for kind in range(2):
        for g in range(EXPERTS):

            @pl.when(host_of(g)[0] != me)
            def _():
                row_copy(kind, g)[1].wait_send()

    for copy in residuals:
        copy.wait_send()
    for place in range(4):
        for index in range(3):
            sibling_copy(place, index).wait_send()
    for n in range(2):
        for index in range(3):
            host_copy(n, index).wait_send()
    for q in range(n_src):
        back_copy(q, *up_args).wait_send()
        back_copy(q, *dn_args).wait_send()


def per_device(
    act_up, routes_up, gates_up, saved_down, grad_down, routes_down, gates_down, norm_gain, w_gate, w_up, w_down,
):
    tokens, features = act_up.shape[1:]
    hidden = w_gate.shape[3]
    half = features // 2
    rows = EXPERTS * BLOCK
    vmem = pl.BlockSpec(memory_space=pltpu.VMEM)
    hbm = pl.BlockSpec(memory_space=pl.ANY)
    dma = pltpu.SemaphoreType.DMA
    up, down = pl.pallas_call(
        kernel,
        out_shape=(jax.ShapeDtypeStruct((tokens, features), BF16),) * 2,
        in_specs=[vmem] * 8 + [hbm] * 3,
        out_specs=(vmem, vmem),
        scratch_shapes=[
            pltpu.VMEM((SLICES, features, hidden), BF16),
            pltpu.VMEM((SLICES, features, hidden), BF16),
            pltpu.VMEM((SLICES, hidden, features), BF16),
            pltpu.VMEM((2 * tokens, half), BF16),
            pltpu.VMEM((2 * tokens, features), BF16),
            pltpu.VMEM((rows, half), BF16),
            pltpu.VMEM((rows, features), BF16),
            pltpu.VMEM((rows, half), BF16),
            pltpu.VMEM((rows, features), BF16),
            pltpu.VMEM((EXPERTS * CAP, features), BF16),
            pltpu.VMEM((EXPERTS * CAP, features), BF16),
            pltpu.VMEM((EXPERTS * CAP, features), BF16),
            pltpu.VMEM((EXPERTS * CAP, features), F32),
            pltpu.VMEM((EXPERTS * CAP, features), F32),
            pltpu.VMEM((rows, half), BF16),
            pltpu.VMEM((rows, half), BF16),
            pltpu.VMEM((rows, half), BF16),
            pltpu.VMEM((rows, half), BF16),
            pltpu.VMEM((tokens, features), BF16),
            pltpu.VMEM((tokens, features), BF16),
            pltpu.VMEM((tokens, features), BF16),
            pltpu.VMEM((1, features), F32),
            pltpu.VMEM((1, tokens), jnp.int32),
            pltpu.VMEM((1, tokens), F32),
            pltpu.VMEM((1, tokens), jnp.int32),
            pltpu.VMEM((1, tokens), F32),
            dma((2, EXPERTS)),
            dma((2, EXPERTS)),
            dma((3, 2)),
            dma((SLICES, 3, 2)),
            dma((SLICES, 3)),
            dma((2, 3)),
            dma((EXPERTS,)),
            dma((EXPERTS,)),
            dma((EXPERTS,)),
            dma((EXPERTS,)),
            dma((8,)),
            dma((8,)),
        ],
        compiler_params=pltpu.CompilerParams(
            collective_id=0, has_side_effects=True, vmem_limit_bytes=60 * MIB
        ),
        cost_estimate=pl.CostEstimate(flops=12_000_000_000, bytes_accessed=12_000_000, transcendentals=400_000),
    )(
        act_up[0], saved_down[0], grad_down[0], norm_gain,
        routes_up.reshape(1, tokens), gates_up.reshape(1, tokens),
        routes_down.reshape(1, tokens), gates_down.reshape(1, tokens),
        w_gate[0, 0], w_up[0, 0], w_down[0, 0],
    )
    return up[None], down[None]


def solution(mesh):
    tokens = P("section", "expert", None)
    weights = P("section", "expert", None, None)
    return jax.shard_map(
        per_device,
        mesh=mesh,
        in_specs=(tokens,) * 7 + (P("section", None),) + (weights,) * 3,
        out_specs=(tokens, tokens),
        check_vma=False,
    )
```
